32 devices in a mesh: groups: 2 (over y), tensor: 8 (over z, x), dp: 2 (over core).
Axes of the slice: x: 2, y: 2, z: 4, core: 2. Of those that a mesh axis runs over, the one named last changes fastest.
Arguments:
- tokens: bfloat16 [2048, 4096], P(('groups', 'tensor', 'dp')), parts along dimension 0, may hold values from -6 to 6
- norm_gain: float32 [4096], replicated, may hold values from 0.5 to 1.5
- gate_codes: bfloat16 [4096, 28672], P(None, 'tensor'), may hold values from -127 to 127, as said below
- gate_scales: float32 [32, 28672], P(None, 'tensor'), may hold values from 0.00010625 to 0.000421875
- up_codes: bfloat16 [4096, 28672], P(None, 'tensor'), may hold values from -127 to 127, as said below
- up_scales: float32 [32, 28672], P(None, 'tensor'), may hold values from 0.00010625 to 0.000421875
- down_codes: bfloat16 [28672, 4096], P('tensor'), may hold values from -127 to 127, as said below
- down_scales: float32 [1024, 4096], P('tensor'), may hold values from 4.0158724e-05 to 0.00015945376
Outputs:
- layer_out: bfloat16 [2048, 4096], P(('groups', 'tensor', 'dp')), parts along dimension 0
The draws below stay inside these ranges and needn't reach their ends.
There are 2 independent parts, one for each index of `groups`. The reference program is written for one: setup_inputs(seed, part) draws one part's arguments, and reference() takes and returns one part's arrays. A program takes and returns all parts, laid end to end along the dimension named above; an argument that names none is the same for every part. Nothing has to cross between parts.
Inputs may be any that keep to these rules, and one draw needn't show every extreme that they name: `gate_codes`: every entry is a whole number. `up_codes`: every entry is a whole number. `down_codes`: every entry is a whole number.
All inputs are finite; a program needn't handle non-finite values.
Results may differ from the reference program's by a relative error of at most 0.012.
Values may be sent and summed in bfloat16 or wider, within the bound.
No kernel may reach another device: no remote copies, remote signals or barrier semaphores. Data moves between devices by JAX's collectives and lax.ppermute only.
A program may use at most 320 MiB of HBM per device.

```python
import math
import jax
import jax.numpy as jnp
from jax import lax

D = 4096
WALSH = 1024
HB = 28
QBLOCK = 128
FF = 28672
TOKENS = 1024


def draw_gate_codes(key, part):
    return jax.random.randint(jax.random.fold_in(key, 11), (D, FF), -127, 128).astype(jnp.bfloat16)


def draw_up_codes(key, part):
    return jax.random.randint(jax.random.fold_in(key, 23), (D, FF), -127, 128).astype(jnp.bfloat16)


def draw_down_codes(key, part):
    return jax.random.randint(jax.random.fold_in(key, 37), (FF, D), -127, 128).astype(jnp.bfloat16)


def steps_of(stream_key, shape, cuts, smallest, high):
    gain, own = 1.0, jax.random.fold_in(stream_key, 6)
    for axis_at, blocks in cuts:
        draws = jnp.exp(jax.random.uniform(jax.random.fold_in(own, axis_at), (blocks,), jnp.float32, smallest / len(cuts), high / len(cuts)))
        gain = gain * jnp.repeat(draws, shape[axis_at] // blocks).reshape([-1 if axis == axis_at else 1 for axis in range(len(shape))])
    return gain


def centred(key, shape, scale, bound, pieces=(), kind=jnp.bfloat16):
    loudness = steps_of(key, shape, pieces, -0.22, 0.18) if pieces else 1.0
    result = jax.random.normal(key, shape, jnp.float32) * scale * loudness
    return jnp.minimum(jnp.maximum(result, -bound), bound).astype(kind)


def setup_inputs(seed: int = 0, part: int = 0) -> dict:
    arg_keys = jax.random.split(jax.random.key(seed), 9)
    part_splits = jax.random.split(jax.random.fold_in(arg_keys[8], part), 9)
    return {
        "tokens": centred(part_splits[0], (TOKENS, D), 1.0, 6.0, ((0, 16),)),
        "norm_gain": jnp.clip(1.0 + 0.1 * jax.random.normal(arg_keys[1], (D,), jnp.float32), 0.5, 1.5),
        "gate_codes": draw_gate_codes(jax.random.fold_in(arg_keys[8], 71), part),
        "gate_scales": jnp.clip(jnp.exp(math.log(0.000421875) - 1.37891427 * jax.random.uniform(arg_keys[3], (D // QBLOCK, FF), jnp.float32) ** steps_of(arg_keys[3], (D // QBLOCK, FF), ((1, 8),), -0.2, 0.2)), 0.00010625, 0.000421875),
        "up_codes": draw_up_codes(jax.random.fold_in(arg_keys[8], 71), part),
        "up_scales": jnp.clip(jnp.exp(math.log(0.000421875) - 1.37891427 * jax.random.uniform(arg_keys[5], (D // QBLOCK, FF), jnp.float32) ** steps_of(arg_keys[5], (D // QBLOCK, FF), ((1, 8),), -0.2, 0.2)), 0.00010625, 0.000421875),
        "down_codes": draw_down_codes(jax.random.fold_in(arg_keys[8], 71), part),
        "down_scales": jnp.clip(jnp.exp(math.log(0.00015945376) - 1.37891428 * jax.random.uniform(arg_keys[7], (WALSH, D), jnp.float32) ** steps_of(arg_keys[7], (WALSH, D), ((0, 8),), -0.2, 0.2)), 4.015872400486842e-05, 0.00015945376),
    }


EPSILON = 1e-05

def hadamard_small():
    modulus = 13
    residues = [number * number % modulus for number in range(1, modulus)]
    legendre = [0] + [1 if number in residues else -1 for number in range(1, modulus)]
    plus_block = [[1, 1], [1, -1]]
    zero_block = [[1, -1], [-1, -1]]

    def conference_entry(row_number, column_number):
        if row_number == 0 and column_number == 0:
            return 0
        if row_number == 0 or column_number == 0:
            return 1
        return legendre[(column_number - row_number) % modulus]
    table = [[conference_entry(row_block, column_block) * plus_block[row_inner][column_inner] + (zero_block[row_inner][column_inner] if row_block == column_block else 0) for column_block in range(modulus + 1) for column_inner in range(2)] for row_block in range(modulus + 1) for row_inner in range(2)]
    return jnp.asarray(table, jnp.float32)

def walsh(order):
    counter = jnp.arange(order, dtype=jnp.int32)
    common = counter[:, None] & counter[None, :]
    parity = jnp.zeros((order, order), jnp.int32)
    for level in range(order.bit_length() - 1):
        parity = parity + (common >> level & 1)
    return (1 - 2 * (parity % 2)).astype(jnp.float32)

def dequantize(codes, scales):
    blocks = scales.shape[0]
    height = codes.shape[0]
    width = codes.shape[1]
    spread = codes.astype(jnp.float32).reshape(blocks, height // blocks, width) * scales[:, None, :]
    return spread.reshape(height, width).astype(jnp.bfloat16)

def rotate(hidden):
    height = hidden.shape[0]
    blocks = hidden.astype(jnp.float32).reshape(height, WALSH, HB)
    small_table = hadamard_small()
    blocks = jnp.einsum('tia,ac->tic', blocks, small_table, precision=lax.Precision.HIGHEST)
    blocks = jnp.einsum('ji,tic->tjc', walsh(WALSH), blocks, precision=lax.Precision.HIGHEST)
    return (blocks * FF ** (-0.5)).reshape(height, FF).astype(jnp.bfloat16)

def reference(tokens, norm_gain, gate_codes, gate_scales, up_codes, up_scales, down_codes, down_scales):
    floated = tokens.astype(jnp.float32)
    normed = (floated * lax.rsqrt(lax.optimization_barrier(jnp.mean(floated * floated, axis=1, keepdims=True)) + EPSILON) * norm_gain).astype(jnp.bfloat16)
    gate_weight = dequantize(gate_codes, gate_scales)
    up_weight = dequantize(up_codes, up_scales)
    down_weight = dequantize(down_codes, down_scales)
    gate = jnp.dot(normed, gate_weight, preferred_element_type=jnp.float32)
    upward = jnp.dot(normed, up_weight, preferred_element_type=jnp.float32)
    hidden = (jax.nn.silu(gate) * upward).astype(jnp.bfloat16)
    rotated = rotate(hidden)
    down = jnp.dot(rotated, down_weight, preferred_element_type=jnp.float32)
    return (floated + down).astype(jnp.bfloat16)
```

```python
import functools
import math

import jax
import jax.numpy as jnp
import ml_dtypes
import numpy as np
from jax import lax
from jax.experimental import pallas as pl
from jax.experimental.pallas import tpu as pltpu
from jax.sharding import PartitionSpec as P

EPSILON = 1e-05
AXIS = "tensor"
MIB = 1 << 20


def hadamard_small():
    modulus = 13
    residues = [number * number % modulus for number in range(1, modulus)]
    legendre = [0] + [1 if number in residues else -1 for number in range(1, modulus)]
    conference = np.zeros((modulus + 1, modulus + 1), np.int64)
    conference[0, 1:] = 1
    conference[1:, 0] = 1
    for row in range(1, modulus + 1):
        for column in range(1, modulus + 1):
            conference[row, column] = legendre[(column - row) % modulus]
    plus_block = np.array([[1, 1], [1, -1]])
    zero_block = np.array([[1, -1], [-1, -1]])
    return np.kron(conference, plus_block) + np.kron(np.eye(modulus + 1, dtype=np.int64), zero_block)


def walsh(order):
    table = np.ones((1, 1), np.int64)
    while table.shape[0] < order:
        table = np.kron(np.array([[1, 1], [1, -1]]), table)
    return table


def exchange(value, stride):
    return lax.ppermute(value, AXIS, [(i, i ^ stride) for i in range(lax.axis_size(AXIS))])


def gather_pieces(own, devices):
    pieces = {0: own}
    order = sorted(range(1, devices), key=lambda k: (bin(k).count("1"), -k))
    for k in order:
        low = k & -k
        pieces[k] = exchange(pieces[k ^ low], low)
    return [pieces[k] for k in range(devices)]


def swap_pieces(pieces):
    devices = len(pieces)
    out = list(pieces)
    for k in range(devices - 1, 0, -1):
        out[k] = exchange(pieces[k], k)
    return out


def reversed_bits(k, devices):
    levels = devices.bit_length() - 1
    return sum(((k >> level) & 1) << (levels - 1 - level) for level in range(levels))


def norm_kernel(cuts, tokens_ref, gain_ref, *out_refs):
    floated = tokens_ref[...].astype(jnp.float32)
    inverse = lax.rsqrt(jnp.mean(floated * floated, axis=1, keepdims=True) + EPSILON)
    normed = (floated * inverse * gain_ref[...]).astype(jnp.bfloat16)
    for (start, rows), out_ref in zip(cuts, out_refs):
        out_ref[...] = normed[start : start + rows]


def norm(tokens, gain, cuts):
    rows, width = tokens.shape
    return pl.pallas_call(
        functools.partial(norm_kernel, cuts),
        out_shape=[jax.ShapeDtypeStruct((count, width), jnp.bfloat16) for _, count in cuts],
        compiler_params=pltpu.CompilerParams(vmem_limit_bytes=16 * MIB),
        cost_estimate=pl.CostEstimate(
            flops=5 * rows * width, bytes_accessed=4 * rows * width, transcendentals=rows
        ),
        name="norm",
    )(tokens, gain.reshape(1, width))


def gate_up_kernel(devices, depth, qblock, *refs):
    piece_refs = refs[:devices]
    gate_ref, gate_scale_ref, up_ref, up_scale_ref = refs[devices : devices + 4]
    out_refs = refs[devices + 4 : 2 * devices + 4]
    held = refs[2 * devices + 4]
    rows = piece_refs[0].shape[0]

    @pl.when(pl.program_id(0) == 0)
    def _():
        for k in range(devices):
            held[k * rows : (k + 1) * rows, :] = piece_refs[k][...]

    def weight(code_ref, scale_ref, at):
        parts = []
        for block in range(at // qblock, (at + depth) // qblock):
            codes = code_ref[block * qblock : (block + 1) * qblock, :].astype(jnp.float32)
            parts.append((codes * scale_ref[block : block + 1, :]).astype(jnp.bfloat16))
        return jnp.concatenate(parts, axis=0)

    gate = up = None
    for at in range(0, gate_ref.shape[0], depth):
        left = held[:, at : at + depth]
        term = jnp.dot(left, weight(gate_ref, gate_scale_ref, at), preferred_element_type=jnp.float32)
        gate = term if gate is None else gate + term
        term = jnp.dot(left, weight(up_ref, up_scale_ref, at), preferred_element_type=jnp.float32)
        up = term if up is None else up + term
    hidden = (gate / (1.0 + jnp.exp(-gate)) * up).astype(jnp.bfloat16)
    for k in range(devices):
        out_refs[k][...] = hidden[k * rows : (k + 1) * rows]


def gate_up(pieces, gate_codes, gate_scales, up_codes, up_scales):
    devices = len(pieces)
    rows, width = pieces[0].shape
    local = gate_codes.shape[1]
    blocks = gate_scales.shape[0]
    tile = 256
    codes = pl.BlockSpec((width, tile), lambda i: (0, i))
    scales = pl.BlockSpec((blocks, tile), lambda i: (0, i))
    return pl.pallas_call(
        functools.partial(gate_up_kernel, devices, 512, width // blocks),
        grid=(local // tile,),
        in_specs=[pl.BlockSpec((rows, width), lambda i: (0, 0))] * devices
        + [codes, scales, codes, scales],
        out_specs=[pl.BlockSpec((rows, tile), lambda i: (0, i))] * devices,
        out_shape=[jax.ShapeDtypeStruct((rows, local), jnp.bfloat16)] * devices,
        scratch_shapes=[pltpu.VMEM((devices * rows, width), jnp.bfloat16)],
        compiler_params=pltpu.CompilerParams(
            dimension_semantics=("arbitrary",), vmem_limit_bytes=40 * MIB
        ),
        cost_estimate=pl.CostEstimate(
            flops=4 * devices * rows * width * local,
            bytes_accessed=4 * width * local,
            transcendentals=devices * rows * local,
        ),
        name="gate_up",
    )(*pieces, gate_codes, gate_scales, up_codes, up_scales)


def rotate_kernel(devices, factor, sign_ref, *refs):
    piece_refs = refs[:devices]
    table_ref = refs[devices]
    out_refs = refs[devices + 1 : 2 * devices + 1]
    held = refs[2 * devices + 1]
    rows, local = piece_refs[0].shape
    block = table_ref.shape[0]
    inner = local // block
    count = devices * inner
    for k in range(devices):
        sign = sign_ref[0, k].astype(jnp.bfloat16)
        for q in range(inner):
            at = (k * inner + q) * rows
            held[at : at + rows, :] = piece_refs[k][:, q * block : (q + 1) * block] * sign
    for start in range(0, block, 256):
        stop = min(start + 256, block)
        product = jnp.dot(
            held[...], table_ref[:, start:stop], preferred_element_type=jnp.float32
        )
        values = [product[index * rows : (index + 1) * rows] for index in range(count)]
        stride = 1
        while stride < count:
            values = [
                values[index] + values[index ^ stride]
                if not index & stride
                else values[index ^ stride] - values[index]
                for index in range(count)
            ]
            stride *= 2
        for k in range(devices):
            scale = sign_ref[1, k] * factor
            for q in range(inner):
                out_refs[k][:, q * block + start : q * block + stop] = (
                    values[k * inner + q] * scale
                ).astype(jnp.bfloat16)


def rotate(pieces, signs, table):
    devices = len(pieces)
    rows, local = pieces[0].shape
    block = table.shape[0]
    vmem = pl.BlockSpec(memory_space=pltpu.VMEM)
    return pl.pallas_call(
        functools.partial(rotate_kernel, devices, (devices * local) ** (-0.5)),
        in_specs=[pl.BlockSpec(memory_space=pltpu.SMEM)] + [vmem] * (devices + 1),
        out_specs=[vmem] * devices,
        out_shape=[jax.ShapeDtypeStruct((rows, local), jnp.bfloat16)] * devices,
        scratch_shapes=[pltpu.VMEM((devices * rows * local // block, block), jnp.bfloat16)],
        compiler_params=pltpu.CompilerParams(vmem_limit_bytes=40 * MIB),
        cost_estimate=pl.CostEstimate(
            flops=2 * devices * rows * local * block,
            bytes_accessed=4 * devices * rows * local,
            transcendentals=0,
        ),
        name="rotate",
    )(signs, *pieces, table)


def down_kernel(devices, group, order, *refs):
    piece_refs = refs[:devices]
    code_ref, scale_ref, keep_ref, send_ref, held, weight = refs[devices:]
    rows, local = piece_refs[0].shape
    half = devices // 2

    @pl.when(pl.program_id(0) == 0)
    def _():
        for place, k in enumerate(order):
            held[place * rows : (place + 1) * rows, :] = piece_refs[k][...]

    tile = code_ref.shape[1]
    repeat = math.lcm(group, 16)
    low_rows = lax.broadcasted_iota(jnp.int32, (8, tile), 0)
    parts = 2 if local % (2 * repeat) == 0 and local % 512 == 0 else 1
    depth = local // parts
    total = None
    for part in range(parts):
        for at in range(part * depth, (part + 1) * depth, repeat):
            steps = []
            for row in range(at, at + repeat, 8):
                first, last = row // group, (row + 7) // group
                step = jnp.broadcast_to(scale_ref[first : first + 1, :], (8, tile))
                if last != first:
                    other = jnp.broadcast_to(scale_ref[last : last + 1, :], (8, tile))
                    step = jnp.where(low_rows < last * group - row, step, other)
                steps.append(step)
            codes = code_ref[at : at + repeat, :].astype(jnp.float32)
            weight[at : at + repeat, :] = (codes * jnp.concatenate(steps, axis=0)).astype(
                jnp.bfloat16
            )
        term = jnp.dot(
            held[:, part * depth : (part + 1) * depth],
            weight[part * depth : (part + 1) * depth, :],
            preferred_element_type=jnp.float32,
        )
        total = term if total is None else total + term
    keep_ref[...] = total[: half * rows]
    send_ref[...] = total[half * rows :].astype(jnp.bfloat16)


def down(pieces, codes, scales):
    devices = len(pieces)
    rows, local = pieces[0].shape
    width = codes.shape[1]
    blocks = scales.shape[0]
    tile = 512
    order = sorted(range(devices), key=lambda k: reversed_bits(k, devices))
    out_rows = devices // 2 * rows
    return pl.pallas_call(
        functools.partial(down_kernel, devices, local // blocks, order),
        grid=(width // tile,),
        in_specs=[pl.BlockSpec((rows, local), lambda i: (0, 0))] * devices
        + [
            pl.BlockSpec((local, tile), lambda i: (0, i)),
            pl.BlockSpec((blocks, tile), lambda i: (0, i)),
        ],
        out_specs=[pl.BlockSpec((out_rows, tile), lambda i: (0, i))] * 2,
        out_shape=[
            jax.ShapeDtypeStruct((out_rows, width), jnp.float32),
            jax.ShapeDtypeStruct((out_rows, width), jnp.bfloat16),
        ],
        scratch_shapes=[
            pltpu.VMEM((devices * rows, local), jnp.bfloat16),
            pltpu.VMEM((local, tile), jnp.bfloat16),
        ],
        compiler_params=pltpu.CompilerParams(
            dimension_semantics=("arbitrary",), vmem_limit_bytes=40 * MIB
        ),
        cost_estimate=pl.CostEstimate(
            flops=2 * devices * rows * width * local,
            bytes_accessed=2 * width * local,
            transcendentals=0,
        ),
        name="down",
    )(*pieces, codes, scales)


def sum_over_devices(keep, send):
    stride = 1
    while True:
        got = exchange(send, stride)
        total = keep + got.astype(jnp.float32)
        rows = total.shape[0]
        stride *= 2
        if stride == lax.axis_size(AXIS):
            return total
        keep, send = total[: rows // 2], total[rows // 2 :].astype(jnp.bfloat16)


def block_order(local, group):
    order = local // group
    while order > 32:
        order //= 2
    return order


def shards_piped(
    chunks, tokens, norm_gain, gate_codes, gate_scales, up_codes, up_scales, down_codes, down_scales
):
    devices = lax.axis_size(AXIS)
    local = gate_codes.shape[1]
    group = down_codes.shape[0] // down_scales.shape[0]
    table = np.kron(walsh(block_order(local, group)), hadamard_small())
    table = jnp.asarray(table.astype(ml_dtypes.bfloat16))

    grid = walsh(devices)
    both = np.stack(
        [[grid[me], [grid[me ^ k, me] for k in range(devices)]] for me in range(devices)]
    )
    signs = lax.dynamic_index_in_dim(
        jnp.asarray(both, jnp.float32), lax.axis_index(AXIS), 0, keepdims=False
    )

    own = norm(tokens, norm_gain, chunks)
    gathered = [gather_pieces(piece, devices) for piece in own]
    hidden = [
        swap_pieces(gate_up(pieces, gate_codes, gate_scales, up_codes, up_scales))
        for pieces in gathered
    ]
    rotated = [swap_pieces(rotate(pieces, signs, table)) for pieces in hidden]
    summed = [sum_over_devices(*down(pieces, down_codes, down_scales)) for pieces in rotated]
    outs = [
        (tokens[start : start + rows].astype(jnp.float32) + total).astype(jnp.bfloat16)
        for (start, rows), total in zip(chunks, summed)
    ]
    return jnp.concatenate(outs, axis=0)


def dequantize(codes, scales):
    blocks = scales.shape[0]
    height, width = codes.shape
    spread = codes.astype(jnp.float32).reshape(blocks, height // blocks, width) * scales[:, None, :]
    return spread.reshape(height, width).astype(jnp.bfloat16)


def shards_plain(
    tokens, norm_gain, gate_codes, gate_scales, up_codes, up_scales, down_codes, down_scales
):
    floated = tokens.astype(jnp.float32)
    normed = (
        floated
        * lax.rsqrt(jnp.mean(floated * floated, axis=1, keepdims=True) + EPSILON)
        * norm_gain
    ).astype(jnp.bfloat16)
    gate_weight = dequantize(gate_codes, gate_scales)
    up_weight = dequantize(up_codes, up_scales)
    down_weight = dequantize(down_codes, down_scales)
    piece = lax.all_gather(normed, AXIS, axis=0, tiled=True)
    gate = jnp.dot(piece, gate_weight, preferred_element_type=jnp.float32)
    upward = jnp.dot(piece, up_weight, preferred_element_type=jnp.float32)
    hidden = (jax.nn.silu(gate) * upward).astype(jnp.bfloat16)
    total_rows, local_width = hidden.shape
    devices = lax.axis_size(AXIS)
    local_walsh = down_scales.shape[0]
    group = down_codes.shape[0] // local_walsh
    blocks = hidden.astype(jnp.float32).reshape(total_rows, local_walsh, group)
    small_table = jnp.asarray(hadamard_small(), jnp.float32)
    local_table = jnp.asarray(walsh(local_walsh), jnp.float32)
    blocks = jnp.einsum("tia,ac->tic", blocks, small_table, precision=lax.Precision.HIGHEST)
    blocks = jnp.einsum("ji,tic->tjc", local_table, blocks, precision=lax.Precision.HIGHEST)
    blocks = blocks.reshape(total_rows, local_width)
    position = lax.axis_index(AXIS)
    for level in range(devices.bit_length() - 1):
        partner = exchange(blocks.astype(jnp.bfloat16), 1 << level).astype(blocks.dtype)
        signed = (1 - 2 * (position >> level & 1)).astype(jnp.float32)
        blocks = partner + signed * blocks
    rotated = (blocks * (devices * local_width) ** (-0.5)).astype(jnp.bfloat16)
    summed = lax.psum_scatter(
        jnp.dot(rotated, down_weight, preferred_element_type=jnp.float32),
        AXIS,
        scatter_dimension=0,
        tiled=True,
    )
    return (floated + summed).astype(jnp.bfloat16)


CHUNKS = 2


def shards(tokens, norm_gain, gate_codes, *others):
    devices = lax.axis_size(AXIS)
    rows, width = tokens.shape
    local = gate_codes.shape[1]
    if devices in (2, 4, 8) and rows % (16 * CHUNKS) == 0 and local % 896 == 0 and width % 512 == 0:
        size = rows // CHUNKS
        chunks = [(index * size, size) for index in range(CHUNKS)]
        return shards_piped(chunks, tokens, norm_gain, gate_codes, *others)
    return shards_plain(tokens, norm_gain, gate_codes, *others)


def solution(mesh):
    return jax.shard_map(
        shards,
        mesh=mesh,
        in_specs=(
            P(("groups", "tensor", "dp"), None),
            P(),
            P(None, "tensor"),
            P(None, "tensor"),
            P(None, "tensor"),
            P(None, "tensor"),
            P("tensor", None),
            P("tensor", None),
        ),
        out_specs=P(("groups", "tensor", "dp"), None),
        check_vma=False,
    )
```

```python
import functools
import math

import jax
import jax.numpy as jnp
import ml_dtypes
import numpy as np
from jax import lax
from jax.experimental import pallas as pl
from jax.experimental.pallas import tpu as pltpu
from jax.sharding import PartitionSpec as P

EPSILON = 1e-05
AXIS = "tensor"
MIB = 1 << 20


def hadamard_small():
    modulus = 13
    residues = [number * number % modulus for number in range(1, modulus)]
    legendre = [0] + [1 if number in residues else -1 for number in range(1, modulus)]
    conference = np.zeros((modulus + 1, modulus + 1), np.int64)
    conference[0, 1:] = 1
    conference[1:, 0] = 1
    for row in range(1, modulus + 1):
        for column in range(1, modulus + 1):
            conference[row, column] = legendre[(column - row) % modulus]
    plus_block = np.array([[1, 1], [1, -1]])
    zero_block = np.array([[1, -1], [-1, -1]])
    return np.kron(conference, plus_block) + np.kron(np.eye(modulus + 1, dtype=np.int64), zero_block)


def walsh(order):
    table = np.ones((1, 1), np.int64)
    while table.shape[0] < order:
        table = np.kron(np.array([[1, 1], [1, -1]]), table)
    return table


def exchange(value, stride):
    return lax.ppermute(value, AXIS, [(i, i ^ stride) for i in range(lax.axis_size(AXIS))])


def after(value, *earlier):
    return lax.optimization_barrier((value, earlier))[0]


def reversed_bits(k, devices):
    levels = devices.bit_length() - 1
    return sum(((k >> level) & 1) << (levels - 1 - level) for level in range(levels))


def gather_tree(own, devices):
    pieces = {0: own}
    for k in sorted(range(1, devices), key=lambda k: (bin(k).count("1"), -k)):
        low = k & -k
        pieces[k] = exchange(pieces[k ^ low], low)
    return [(pieces[k], 0) for k in range(devices)]


def gather_step(held, stride):
    return jnp.concatenate([held, exchange(held, stride)], axis=0)


def gathered_pieces(near, far, devices, rows, start):
    half = devices // 2
    places = [reversed_bits(k, devices) for k in range(devices)]
    return [
        (near, place * rows + start) if place < half else (far, (place - half) * rows + start)
        for place in places
    ]


def swap_far(arrays):
    out = list(arrays)
    for j in range(len(arrays) - 1, 0, -1):
        out[j] = exchange(arrays[j], 2 * j)
    return out


def swap_near(arrays):
    rows = arrays[0].shape[0] // 2
    came = exchange(jnp.concatenate([array[rows:] for array in arrays], axis=0), 1)
    pieces = []
    for j, array in enumerate(arrays):
        pieces += [(array, 0), (came, j * rows)]
    return pieces


def swap_direct(arrays):
    out = list(arrays)
    for k in range(len(arrays) - 1, 0, -1):
        out[k] = exchange(arrays[k], k)
    return [(array, 0) for array in out]


def distinct(pieces):
    arrays, places = [], []
    for array, start in pieces:
        at = next((i for i, other in enumerate(arrays) if other is array), len(arrays))
        if at == len(arrays):
            arrays.append(array)
        places.append((at, start))
    return arrays, places


def whole_blocks(arrays):
    return [pl.BlockSpec(array.shape, lambda i: (0, 0)) for array in arrays]


def norm_kernel(cuts, tokens_ref, gain_ref, *out_refs):
    floated = tokens_ref[...].astype(jnp.float32)
    inverse = lax.rsqrt(jnp.mean(floated * floated, axis=1, keepdims=True) + EPSILON)
    normed = (floated * inverse * gain_ref[...]).astype(jnp.bfloat16)
    for (start, rows), out_ref in zip(cuts, out_refs):
        out_ref[...] = normed[start : start + rows]


def norm(tokens, gain, cuts):
    rows, width = tokens.shape
    return pl.pallas_call(
        functools.partial(norm_kernel, cuts),
        out_shape=[jax.ShapeDtypeStruct((count, width), jnp.bfloat16) for _, count in cuts],
        compiler_params=pltpu.CompilerParams(vmem_limit_bytes=16 * MIB),
        cost_estimate=pl.CostEstimate(
            flops=5 * rows * width, bytes_accessed=4 * rows * width, transcendentals=rows
        ),
        name="norm",
    )(tokens, gain.reshape(1, width))


def gate_up_kernel(places, rows, depth, qblock, ins, *refs):
    devices = len(places)
    piece_refs = refs[:ins]
    gate_ref, gate_scale_ref, up_ref, up_scale_ref = refs[ins : ins + 4]
    out_refs = refs[ins + 4 : -1]
    held = refs[-1]

    @pl.when(pl.program_id(0) == 0)
    def _():
        for k, (at, start) in enumerate(places):
            held[k * rows : (k + 1) * rows, :] = piece_refs[at][start : start + rows, :]

    def weight(code_ref, scales, at):
        parts = []
        for block in range(at // qblock, (at + depth) // qblock):
            codes = code_ref[block * qblock : (block + 1) * qblock, :]
            parts.append(codes * scales[block : block + 1, :])
        return jnp.concatenate(parts, axis=0)

    gate_scales = gate_scale_ref[...].astype(jnp.bfloat16)
    up_scales = up_scale_ref[...].astype(jnp.bfloat16)
    gate = up = None
    for at in range(0, gate_ref.shape[0], depth):
        left = held[:, at : at + depth]
        term = jnp.dot(left, weight(gate_ref, gate_scales, at), preferred_element_type=jnp.float32)
        gate = term if gate is None else gate + term
        term = jnp.dot(left, weight(up_ref, up_scales, at), preferred_element_type=jnp.float32)
        up = term if up is None else up + term
    hidden = (gate / (1.0 + jnp.exp(-gate)) * up).astype(jnp.bfloat16)
    per = devices // len(out_refs)
    for index, out_ref in enumerate(out_refs):
        out_ref[...] = hidden[index * per * rows : (index + 1) * per * rows]


def gate_up(pieces, rows, per, gate_codes, gate_scales, up_codes, up_scales):
    devices = len(pieces)
    arrays, places = distinct(pieces)
    width, local = gate_codes.shape
    blocks = gate_scales.shape[0]
    tile = 256
    codes = pl.BlockSpec((width, tile), lambda i: (0, i))
    scales = pl.BlockSpec((blocks, tile), lambda i: (0, i))
    return pl.pallas_call(
        functools.partial(gate_up_kernel, places, rows, 1024, width // blocks, len(arrays)),
        grid=(local // tile,),
        in_specs=whole_blocks(arrays) + [codes, scales, codes, scales],
        out_specs=[pl.BlockSpec((per * rows, tile), lambda i: (0, i))] * (devices // per),
        out_shape=[jax.ShapeDtypeStruct((per * rows, local), jnp.bfloat16)] * (devices // per),
        scratch_shapes=[pltpu.VMEM((devices * rows, width), jnp.bfloat16)],
        compiler_params=pltpu.CompilerParams(
            dimension_semantics=("arbitrary",), vmem_limit_bytes=40 * MIB
        ),
        cost_estimate=pl.CostEstimate(
            flops=4 * devices * rows * width * local,
            bytes_accessed=4 * width * local,
            transcendentals=devices * rows * local,
        ),
        name="gate_up",
    )(*arrays, gate_codes, gate_scales, up_codes, up_scales)


def rotate_kernel(places, rows, factor, ins, sign_ref, *refs):
    devices = len(places)
    piece_refs = refs[:ins]
    table_ref = refs[ins]
    out_refs = refs[ins + 1 : -1]
    held = refs[-1]
    local = piece_refs[0].shape[1]
    block = table_ref.shape[0]
    inner = local // block
    count = devices * inner
    per = devices // len(out_refs)
    for k, (source, start) in enumerate(places):
        sign = sign_ref[0, k].astype(jnp.bfloat16)
        for q in range(inner):
            at = (k * inner + q) * rows
            held[at : at + rows, :] = (
                piece_refs[source][start : start + rows, q * block : (q + 1) * block] * sign
            )
    for start in range(0, block, 256):
        stop = min(start + 256, block)
        product = jnp.dot(
            held[...], table_ref[:, start:stop], preferred_element_type=jnp.float32
        )
        values = [product[index * rows : (index + 1) * rows] for index in range(count)]
        stride = 1
        while stride < count:
            values = [
                values[index] + values[index ^ stride]
                if not index & stride
                else values[index ^ stride] - values[index]
                for index in range(count)
            ]
            stride *= 2
        for k in range(devices):
            scale = sign_ref[1, k] * factor
            low = (k % per) * rows
            for q in range(inner):
                out_refs[k // per][low : low + rows, q * block + start : q * block + stop] = (
                    values[k * inner + q] * scale
                ).astype(jnp.bfloat16)


def rotate(pieces, rows, per, signs, table):
    devices = len(pieces)
    arrays, places = distinct(pieces)
    local = arrays[0].shape[1]
    block = table.shape[0]
    vmem = pl.BlockSpec(memory_space=pltpu.VMEM)
    return pl.pallas_call(
        functools.partial(rotate_kernel, places, rows, (devices * local) ** (-0.5), len(arrays)),
        in_specs=[pl.BlockSpec(memory_space=pltpu.SMEM)] + [vmem] * (len(arrays) + 1),
        out_specs=[vmem] * (devices // per),
        out_shape=[jax.ShapeDtypeStruct((per * rows, local), jnp.bfloat16)] * (devices // per),
        scratch_shapes=[pltpu.VMEM((devices * rows * local // block, block), jnp.bfloat16)],
        compiler_params=pltpu.CompilerParams(vmem_limit_bytes=40 * MIB),
        cost_estimate=pl.CostEstimate(
            flops=2 * devices * rows * local * block,
            bytes_accessed=4 * devices * rows * local,
            transcendentals=0,
        ),
        name="rotate",
    )(signs, *arrays, table)


def down_kernel(places, rows, group, order, ins, *refs):
    devices = len(places)
    piece_refs = refs[:ins]
    code_ref, scale_ref, keep_ref, send_ref, held, weight = refs[ins:]
    half = devices // 2

    @pl.when(pl.program_id(0) == 0)
    def _():
        for place, k in enumerate(order):
            at, start = places[k]
            held[place * rows : (place + 1) * rows, :] = piece_refs[at][start : start + rows, :]

    local, tile = code_ref.shape
    pack = 16
    repeat = math.lcm(group, pack)
    pack_rows = lax.broadcasted_iota(jnp.int32, (pack, tile), 0)
    scales = scale_ref[...].astype(jnp.bfloat16)
    masks = {}

    def first_rows(cut):
        if cut not in masks:
            mask = jnp.where(pack_rows < cut, 1.0, 0.0)
            masks[cut] = (mask.astype(jnp.bfloat16), (1.0 - mask).astype(jnp.bfloat16))
        return masks[cut]

    parts = 2 if local % (2 * repeat) == 0 and local % 512 == 0 else 1
    depth = local // parts
    total = None
    for part in range(parts):
        for at in range(part * depth, (part + 1) * depth, repeat):
            steps = []
            for row in range(at, at + repeat, pack):
                first, last = row // group, (row + pack - 1) // group
                step = jnp.broadcast_to(scales[first : first + 1, :], (pack, tile))
                if last != first:
                    head, rest = first_rows(last * group - row)
                    step = step * head + scales[last : last + 1, :] * rest
                steps.append(step)
            weight[at : at + repeat, :] = code_ref[at : at + repeat, :] * jnp.concatenate(
                steps, axis=0
            )
        term = jnp.dot(
            held[:, part * depth : (part + 1) * depth],
            weight[part * depth : (part + 1) * depth, :],
            preferred_element_type=jnp.float32,
        )
        total = term if total is None else total + term
    keep_ref[...] = total[: half * rows]
    send_ref[...] = total[half * rows :].astype(jnp.bfloat16)


def down(pieces, rows, strides, first_column, columns, codes, scales):
    devices = len(pieces)
    arrays, places = distinct(pieces)
    local = codes.shape[0]
    blocks = scales.shape[0]
    tile = 512
    skip = first_column // tile
    levels = len(strides)
    order = sorted(
        range(devices),
        key=lambda k: sum(1 << (levels - 1 - i) for i, stride in enumerate(strides) if k & stride),
    )
    out_rows = devices // 2 * rows
    return pl.pallas_call(
        functools.partial(down_kernel, places, rows, local // blocks, order, len(arrays)),
        grid=(columns // tile,),
        in_specs=whole_blocks(arrays)
        + [
            pl.BlockSpec((local, tile), lambda i: (0, i + skip)),
            pl.BlockSpec((blocks, tile), lambda i: (0, i + skip)),
        ],
        out_specs=[pl.BlockSpec((out_rows, tile), lambda i: (0, i))] * 2,
        out_shape=[
            jax.ShapeDtypeStruct((out_rows, columns), jnp.float32),
            jax.ShapeDtypeStruct((out_rows, columns), jnp.bfloat16),
        ],
        scratch_shapes=[
            pltpu.VMEM((devices * rows, local), jnp.bfloat16),
            pltpu.VMEM((local, tile), jnp.bfloat16),
        ],
        compiler_params=pltpu.CompilerParams(
            dimension_semantics=("arbitrary",), vmem_limit_bytes=40 * MIB
        ),
        cost_estimate=pl.CostEstimate(
            flops=2 * devices * rows * columns * local,
            bytes_accessed=2 * columns * local,
            transcendentals=0,
        ),
        name="down",
    )(*arrays, codes, scales)


def add_step(keep, send, stride):
    total = keep + exchange(send, stride).astype(jnp.float32)
    return total


def split_step(total):
    half = total.shape[0] // 2
    return total[:half], total[half:].astype(jnp.bfloat16)


def block_order(local, group):
    order = local // group
    while order > 32:
        order //= 2
    return order


def shards_piped(
    tokens, norm_gain, gate_codes, gate_scales, up_codes, up_scales, down_codes, down_scales
):
    devices = lax.axis_size(AXIS)
    width = tokens.shape[1]
    local = gate_codes.shape[1]
    group = down_codes.shape[0] // down_scales.shape[0]
    rows = tokens.shape[0] // 4
    table = np.kron(walsh(block_order(local, group)), hadamard_small())
    table = jnp.asarray(table.astype(ml_dtypes.bfloat16))

    grid = walsh(devices)
    both = np.stack(
        [[grid[me], [grid[me ^ k, me] for k in range(devices)]] for me in range(devices)]
    )
    signs = lax.dynamic_index_in_dim(
        jnp.asarray(both, jnp.float32), lax.axis_index(AXIS), 0, keepdims=False
    )
    strides = [1 << level for level in range(devices.bit_length() - 1)]
    weights = (gate_codes, gate_scales, up_codes, up_scales)

    own = norm(tokens, norm_gain, [(0, rows), (rows, rows), (2 * rows, 2 * rows)])
    pieces = [None] * 4
    pieces[0] = gather_tree(own[0], devices)
    pieces[1] = gather_tree(own[1], devices)
    late = after(own[2], pieces[0][-1][0])

    hidden, rotated, sums = [None] * 4, [None] * 4, [None] * 4
    last = None

    def expand(c):
        nonlocal last
        source = [(after(array, last) if last is not None else array, start) for array, start in pieces[c]] \
            if c < 2 else pieces[c]
        if c >= 2 and last is not None:
            arrays, places = distinct(source)
            arrays = after(arrays, last)
            source = [(arrays[at], start) for at, start in places]
        arrays = gate_up(source, rows, 2, *weights)
        last = arrays[0]
        hidden[c] = swap_far(arrays)

    def turn(c):
        nonlocal last
        source = swap_near(hidden[c])
        arrays, places = distinct(source)
        arrays = after(arrays, last)
        direct = c == 3
        arrays = rotate([(arrays[at], start) for at, start in places], rows, 1 if direct else 2, signs, table)
        last = arrays[0]
        rotated[c] = swap_direct(arrays) if direct else swap_far(arrays)

    def contract(c, strides, first_column, columns):
        nonlocal last
        source = rotated[c] if c == 3 else swap_near(rotated[c])
        arrays, places = distinct(source)
        arrays = after(arrays, last)
        keep, send = down(
            [(arrays[at], start) for at, start in places],
            rows,
            strides,
            first_column,
            columns,
            down_codes,
            down_scales,
        )
        last = send
        return keep, send

    def reduce_step(state, stride, final=False):
        nonlocal last
        keep, send = state
        came = after(exchange(send, stride), last)
        total = keep + came.astype(jnp.float32)
        if final:
            return total
        state = split_step(total)
        last = state[1]
        return state

    near = late
    expand(0)
    for stride in strides[:0:-1]:
        near = after(near, last) if stride != strides[-1] else near
        near = gather_step(near, stride)
    far = exchange(near, 1)
    for c in (2, 3):
        pieces[c] = gathered_pieces(near, far, devices, 2 * rows, (c - 2) * rows)
    expand(1)
    turn(0)
    expand(2)
    turn(1)
    sums[0] = contract(0, strides, 0, width)
    expand(3)
    sums[0] = reduce_step(sums[0], strides[0])
    turn(2)
    sums[0] = reduce_step(sums[0], strides[1])
    sums[1] = contract(1, strides, 0, width)
    sums[0] = reduce_step(sums[0], strides[2], True)
    turn(3)
    sums[1] = reduce_step(sums[1], strides[0])
    sums[2] = contract(2, strides, 0, width)
    sums[1] = reduce_step(sums[1], strides[1])
    sums[1] = reduce_step(sums[1], strides[2], True)
    sums[2] = reduce_step(sums[2], strides[0])
    half = width // 2
    other = [strides[1], strides[0], strides[2]]
    left = contract(3, strides, 0, half)
    sums[2] = reduce_step(sums[2], strides[1])
    right = contract(3, other, half, half)
    left = reduce_step(left, strides[0])
    right = reduce_step(right, other[0])
    sums[2] = reduce_step(sums[2], strides[2], True)
    left = reduce_step(left, strides[1])
    right = reduce_step(right, other[1])
    left = reduce_step(left, strides[2], True)
    right = reduce_step(right, other[2], True)
    sums[3] = jnp.concatenate([left, right], axis=1)
    total = jnp.concatenate(sums, axis=0)
    return (tokens.astype(jnp.float32) + total).astype(jnp.bfloat16)


def dequantize(codes, scales):
    blocks = scales.shape[0]
    height, width = codes.shape
    spread = codes.astype(jnp.float32).reshape(blocks, height // blocks, width) * scales[:, None, :]
    return spread.reshape(height, width).astype(jnp.bfloat16)


def shards_plain(
    tokens, norm_gain, gate_codes, gate_scales, up_codes, up_scales, down_codes, down_scales
):
    floated = tokens.astype(jnp.float32)
    normed = (
        floated
        * lax.rsqrt(jnp.mean(floated * floated, axis=1, keepdims=True) + EPSILON)
        * norm_gain
    ).astype(jnp.bfloat16)
    gate_weight = dequantize(gate_codes, gate_scales)
    up_weight = dequantize(up_codes, up_scales)
    down_weight = dequantize(down_codes, down_scales)
    piece = lax.all_gather(normed, AXIS, axis=0, tiled=True)
    gate = jnp.dot(piece, gate_weight, preferred_element_type=jnp.float32)
    upward = jnp.dot(piece, up_weight, preferred_element_type=jnp.float32)
    hidden = (jax.nn.silu(gate) * upward).astype(jnp.bfloat16)
    total_rows, local_width = hidden.shape
    devices = lax.axis_size(AXIS)
    local_walsh = down_scales.shape[0]
    group = down_codes.shape[0] // local_walsh
    blocks = hidden.astype(jnp.float32).reshape(total_rows, local_walsh, group)
    small_table = jnp.asarray(hadamard_small(), jnp.float32)
    local_table = jnp.asarray(walsh(local_walsh), jnp.float32)
    blocks = jnp.einsum("tia,ac->tic", blocks, small_table, precision=lax.Precision.HIGHEST)
    blocks = jnp.einsum("ji,tic->tjc", local_table, blocks, precision=lax.Precision.HIGHEST)
    blocks = blocks.reshape(total_rows, local_width)
    position = lax.axis_index(AXIS)
    for level in range(devices.bit_length() - 1):
        partner = exchange(blocks.astype(jnp.bfloat16), 1 << level).astype(blocks.dtype)
        signed = (1 - 2 * (position >> level & 1)).astype(jnp.float32)
        blocks = partner + signed * blocks
    rotated = (blocks * (devices * local_width) ** (-0.5)).astype(jnp.bfloat16)
    summed = lax.psum_scatter(
        jnp.dot(rotated, down_weight, preferred_element_type=jnp.float32),
        AXIS,
        scatter_dimension=0,
        tiled=True,
    )
    return (floated + summed).astype(jnp.bfloat16)


def shards(tokens, norm_gain, gate_codes, *others):
    devices = lax.axis_size(AXIS)
    rows, width = tokens.shape
    local = gate_codes.shape[1]
    if devices == 8 and rows % 64 == 0 and local % 896 == 0 and width % 1024 == 0:
        return shards_piped(tokens, norm_gain, gate_codes, *others)
    return shards_plain(tokens, norm_gain, gate_codes, *others)


def solution(mesh):
    return jax.shard_map(
        shards,
        mesh=mesh,
        in_specs=(
            P(("groups", "tensor", "dp"), None),
            P(),
            P(None, "tensor"),
            P(None, "tensor"),
            P(None, "tensor"),
            P(None, "tensor"),
            P("tensor", None),
            P("tensor", None),
        ),
        out_specs=P(("groups", "tensor", "dp"), None),
        check_vma=False,
    )
```

```python
import functools
import math

import jax
import jax.numpy as jnp
import ml_dtypes
import numpy as np
from jax import lax
from jax.experimental import pallas as pl
from jax.experimental.pallas import tpu as pltpu
from jax.sharding import PartitionSpec as P

EPSILON = 1e-05
AXIS = "tensor"
MIB = 1 << 20


def hadamard_small():
    modulus = 13
    residues = [number * number % modulus for number in range(1, modulus)]
    legendre = [0] + [1 if number in residues else -1 for number in range(1, modulus)]
    conference = np.zeros((modulus + 1, modulus + 1), np.int64)
    conference[0, 1:] = 1
    conference[1:, 0] = 1
    for row in range(1, modulus + 1):
        for column in range(1, modulus + 1):
            conference[row, column] = legendre[(column - row) % modulus]
    plus_block = np.array([[1, 1], [1, -1]])
    zero_block = np.array([[1, -1], [-1, -1]])
    return np.kron(conference, plus_block) + np.kron(np.eye(modulus + 1, dtype=np.int64), zero_block)


def walsh(order):
    table = np.ones((1, 1), np.int64)
    while table.shape[0] < order:
        table = np.kron(np.array([[1, 1], [1, -1]]), table)
    return table


def exchange(value, stride):
    return lax.ppermute(value, AXIS, [(i, i ^ stride) for i in range(lax.axis_size(AXIS))])


def after(value, *earlier):
    return lax.optimization_barrier((value, earlier))[0]


def gather_doubling(own, strides):
    rows = own.shape[0]
    held, places = own, {0: 0}
    for stride in strides[:-1]:
        places.update({k ^ stride: place + len(places) for k, place in places.items()})
        held = jnp.concatenate([held, exchange(held, stride)], axis=0)
    came = exchange(held, strides[-1])
    pieces = {k: (held, place * rows) for k, place in places.items()}
    pieces.update({k ^ strides[-1]: (came, place * rows) for k, place in places.items()})
    return [pieces[k] for k in range(len(pieces))]


def gather_flat_start(own, devices):
    return exchange(own, 1), [own] + [exchange(own, k) for k in range(2, devices, 2)]


def gather_flat_end(near, pieces):
    rows = near.shape[0]
    came = exchange(jnp.concatenate(pieces[1:], axis=0), 1)
    out = []
    for j, piece in enumerate(pieces):
        out += [(piece, 0), (near, 0) if j == 0 else (came, (j - 1) * rows)]
    return out


def swap_far(arrays):
    out = list(arrays)
    for j in range(len(arrays) - 1, 0, -1):
        out[j] = exchange(arrays[j], 2 * j)
    return out


def swap_near(arrays):
    rows = arrays[0].shape[0] // 2
    came = exchange(jnp.concatenate([array[rows:] for array in arrays], axis=0), 1)
    pieces = []
    for j, array in enumerate(arrays):
        pieces += [(array, 0), (came, j * rows)]
    return pieces


def pairs_near_first(arrays):
    *evens, odds = arrays
    rows = odds.shape[0] // len(evens)
    came = exchange(odds, 1)
    return [
        jnp.concatenate([even, came[j * rows : (j + 1) * rows]], axis=0)
        for j, even in enumerate(evens)
    ]


def pair_pieces(arrays):
    return [(array, start) for array in arrays for start in (0, array.shape[0] // 2)]


def swap_direct(arrays):
    out = list(arrays)
    for k in range(1, len(arrays)):
        out[k] = exchange(arrays[k], k)
    return [(array, 0) for array in out]


def single_layout(devices):
    return [(k, 0) for k in range(devices)]


def pairs_layout(devices):
    return [(k // 2, k % 2) for k in range(devices)]


def near_first_layout(devices):
    return [(devices // 2, k // 2) if k % 2 else (k // 2, 0) for k in range(devices)]


def shapes_of(layout, rows, columns):
    counts = [sum(1 for at, _ in layout if at == index) for index in range(1 + max(layout)[0])]
    return [jax.ShapeDtypeStruct((count * rows, columns), jnp.bfloat16) for count in counts]


def all_after(pieces, *earlier):
    arrays, places = distinct(pieces)
    arrays = after(arrays, *earlier)
    return [(arrays[at], start) for at, start in places]


def distinct(pieces):
    arrays = []
    for array, _ in pieces:
        if not any(other is array for other in arrays):
            arrays.append(array)
    index = {id(array): at for at, array in enumerate(arrays)}
    return arrays, [(index[id(array)], start) for array, start in pieces]


SPLIT = 2


def split_blocks(height, tile, skip):
    return [
        pl.BlockSpec((height // SPLIT, tile), functools.partial(lambda part, i: (part, i + skip), part))
        for part in range(SPLIT)
    ]


def whole_blocks(arrays):
    return [pl.BlockSpec(array.shape, lambda i: (0, 0)) for array in arrays]


def norm_kernel(cuts, tokens_ref, gain_ref, *out_refs):
    floated = tokens_ref[...].astype(jnp.float32)
    inverse = lax.rsqrt(jnp.mean(floated * floated, axis=1, keepdims=True) + EPSILON)
    normed = (floated * inverse * gain_ref[...]).astype(jnp.bfloat16)
    for (row, column), out_ref in zip(cuts, out_refs):
        rows, columns = out_ref.shape
        out_ref[...] = normed[row : row + rows, column : column + columns]


def norm(tokens, gain, cuts):
    rows, width = tokens.shape
    return pl.pallas_call(
        functools.partial(norm_kernel, [cut[:2] for cut in cuts]),
        out_shape=[jax.ShapeDtypeStruct(cut[2:], jnp.bfloat16) for cut in cuts],
        compiler_params=pltpu.CompilerParams(vmem_limit_bytes=16 * MIB),
        cost_estimate=pl.CostEstimate(
            flops=5 * rows * width, bytes_accessed=4 * rows * width, transcendentals=rows
        ),
        name="norm",
    )(tokens, gain.reshape(1, width))


def gate_up_kernel(places, devices, rows, depth, qblock, ins, *refs):
    piece_refs = refs[:ins]
    code_refs = refs[ins : ins + 2 * SPLIT]
    gate_scale_ref, up_scale_ref = refs[ins + 2 * SPLIT : ins + 2 * SPLIT + 2]
    out_refs = refs[ins + 2 * SPLIT + 2 : -1]
    held = refs[-1]
    span = code_refs[0].shape[0]

    @pl.when(pl.program_id(0) == 0)
    def _():
        for index, (at, start) in enumerate(places):
            k, columns = index % devices, piece_refs[at].shape[1]
            left = index // devices * columns
            held[k * rows : (k + 1) * rows, left : left + columns] = piece_refs[at][
                start : start + rows, :
            ]

    def weight(refs_of_codes, scales, at):
        parts = []
        for row in range(at, at + depth, qblock):
            codes = refs_of_codes[row // span][row % span : row % span + qblock, :]
            parts.append(codes * scales[row // qblock : row // qblock + 1, :])
        return jnp.concatenate(parts, axis=0)

    gate_scales = gate_scale_ref[...].astype(jnp.bfloat16)
    up_scales = up_scale_ref[...].astype(jnp.bfloat16)
    gate = up = None
    for at in range(0, SPLIT * span, depth):
        left = held[:, at : at + depth]
        right = weight(code_refs[:SPLIT], gate_scales, at)
        term = jnp.dot(left, right, preferred_element_type=jnp.float32)
        gate = term if gate is None else gate + term
        right = weight(code_refs[SPLIT:], up_scales, at)
        term = jnp.dot(left, right, preferred_element_type=jnp.float32)
        up = term if up is None else up + term
    hidden = (gate / (1.0 + jnp.exp(-gate)) * up).astype(jnp.bfloat16)
    per = devices // len(out_refs)
    for index, out_ref in enumerate(out_refs):
        out_ref[...] = hidden[index * per * rows : (index + 1) * per * rows]


def gate_up(pieces, devices, rows, per, gate_codes, gate_scales, up_codes, up_scales):
    arrays, places = distinct(pieces)
    width, local = gate_codes.shape
    blocks = gate_scales.shape[0]
    tile = 256
    codes = split_blocks(width, tile, 0)
    scales = pl.BlockSpec((blocks, tile), lambda i: (0, i))
    return pl.pallas_call(
        functools.partial(
            gate_up_kernel, places, devices, rows, 1024, width // blocks, len(arrays)
        ),
        grid=(local // tile,),
        in_specs=whole_blocks(arrays) + codes + codes + [scales, scales],
        out_specs=[pl.BlockSpec((per * rows, tile), lambda i: (0, i))] * (devices // per),
        out_shape=[jax.ShapeDtypeStruct((per * rows, local), jnp.bfloat16)] * (devices // per),
        scratch_shapes=[pltpu.VMEM((devices * rows, width), jnp.bfloat16)],
        compiler_params=pltpu.CompilerParams(
            dimension_semantics=("arbitrary",), vmem_limit_bytes=40 * MIB
        ),
        cost_estimate=pl.CostEstimate(
            flops=4 * devices * rows * width * local,
            bytes_accessed=4 * width * local,
            transcendentals=devices * rows * local,
        ),
        name="gate_up",
    )(*arrays, *[gate_codes] * SPLIT, *[up_codes] * SPLIT, gate_scales, up_scales)


def rotate_kernel(places, layout, rows, factor, ins, sign_ref, *refs):
    devices = len(places)
    piece_refs = refs[:ins]
    table_ref = refs[ins]
    out_refs = refs[ins + 1 : -1]
    held = refs[-1]
    local = piece_refs[0].shape[1]
    block = table_ref.shape[0]
    inner = local // block
    count = devices * inner
    for k, (source, start) in enumerate(places):
        sign = sign_ref[0, k].astype(jnp.bfloat16)
        for q in range(inner):
            at = (k * inner + q) * rows
            held[at : at + rows, :] = (
                piece_refs[source][start : start + rows, q * block : (q + 1) * block] * sign
            )
    for start in range(0, block, 256):
        stop = min(start + 256, block)
        product = jnp.dot(
            held[...], table_ref[:, start:stop], preferred_element_type=jnp.float32
        )
        values = [product[index * rows : (index + 1) * rows] for index in range(count)]
        stride = 1
        while stride < count:
            values = [
                values[index] + values[index ^ stride]
                if not index & stride
                else values[index ^ stride] - values[index]
                for index in range(count)
            ]
            stride *= 2
        for k in range(devices):
            scale = sign_ref[1, k] * factor
            at, low = layout[k][0], layout[k][1] * rows
            for q in range(inner):
                out_refs[at][low : low + rows, q * block + start : q * block + stop] = (
                    values[k * inner + q] * scale
                ).astype(jnp.bfloat16)


def rotate(pieces, layout, rows, signs, table):
    devices = len(pieces)
    arrays, places = distinct(pieces)
    local = arrays[0].shape[1]
    block = table.shape[0]
    vmem = pl.BlockSpec(memory_space=pltpu.VMEM)
    return pl.pallas_call(
        functools.partial(
            rotate_kernel, places, layout, rows, (devices * local) ** (-0.5), len(arrays)
        ),
        in_specs=[pl.BlockSpec(memory_space=pltpu.SMEM)] + [vmem] * (len(arrays) + 1),
        out_specs=[vmem] * (1 + max(layout)[0]),
        out_shape=shapes_of(layout, rows, local),
        scratch_shapes=[pltpu.VMEM((devices * rows * local // block, block), jnp.bfloat16)],
        compiler_params=pltpu.CompilerParams(vmem_limit_bytes=40 * MIB),
        cost_estimate=pl.CostEstimate(
            flops=2 * devices * rows * local * block,
            bytes_accessed=4 * devices * rows * local,
            transcendentals=devices * rows * local,
        ),
        name="rotate",
    )(signs, *arrays, table)


def down_kernel(places, rows, group, order, ins, *refs):
    devices = len(places)
    piece_refs = refs[:ins]
    code_refs = refs[ins : ins + SPLIT]
    scale_ref, keep_ref, send_ref, held, weight = refs[ins + SPLIT :]
    half = devices // 2

    @pl.when(pl.program_id(0) == 0)
    def _():
        for place, k in enumerate(order):
            at, start = places[k]
            held[place * rows : (place + 1) * rows, :] = piece_refs[at][start : start + rows, :]

    depth, tile = code_refs[0].shape
    pack = 16
    repeat = math.lcm(group, pack)
    pack_rows = lax.broadcasted_iota(jnp.int32, (pack, tile), 0)
    scales = scale_ref[...].astype(jnp.bfloat16)
    masks = {}

    def first_rows(cut):
        if cut not in masks:
            mask = jnp.where(pack_rows < cut, 1.0, 0.0)
            masks[cut] = (mask.astype(jnp.bfloat16), (1.0 - mask).astype(jnp.bfloat16))
        return masks[cut]

    total = None
    for part in range(SPLIT):
        for at in range(part * depth, (part + 1) * depth, repeat):
            steps = []
            for row in range(at, at + repeat, pack):
                first, last = row // group, (row + pack - 1) // group
                step = jnp.broadcast_to(scales[first : first + 1, :], (pack, tile))
                if last != first:
                    head, rest = first_rows(last * group - row)
                    step = step * head + scales[last : last + 1, :] * rest
                steps.append(step)
            low = at - part * depth
            codes = code_refs[part][low : low + repeat, :]
            weight[at : at + repeat, :] = codes * jnp.concatenate(steps, axis=0)
        term = jnp.dot(
            held[:, part * depth : (part + 1) * depth],
            weight[part * depth : (part + 1) * depth, :],
            preferred_element_type=jnp.float32,
        )
        total = term if total is None else total + term
    keep_ref[...] = total[: half * rows]
    send_ref[...] = total[half * rows :].astype(jnp.bfloat16)


def down(pieces, rows, strides, first_column, columns, codes, scales):
    devices = len(pieces)
    arrays, places = distinct(pieces)
    local = codes.shape[0]
    blocks = scales.shape[0]
    tile = 512
    skip = first_column // tile
    levels = len(strides)
    order = sorted(
        range(devices),
        key=lambda k: sum(1 << (levels - 1 - i) for i, stride in enumerate(strides) if k & stride),
    )
    out_rows = devices // 2 * rows
    return pl.pallas_call(
        functools.partial(down_kernel, places, rows, local // blocks, order, len(arrays)),
        grid=(columns // tile,),
        in_specs=whole_blocks(arrays)
        + split_blocks(local, tile, skip)
        + [pl.BlockSpec((blocks, tile), lambda i: (0, i + skip))],
        out_specs=[pl.BlockSpec((out_rows, tile), lambda i: (0, i))] * 2,
        out_shape=[
            jax.ShapeDtypeStruct((out_rows, columns), jnp.float32),
            jax.ShapeDtypeStruct((out_rows, columns), jnp.bfloat16),
        ],
        scratch_shapes=[
            pltpu.VMEM((devices * rows, local), jnp.bfloat16),
            pltpu.VMEM((local, tile), jnp.bfloat16),
        ],
        compiler_params=pltpu.CompilerParams(
            dimension_semantics=("arbitrary",), vmem_limit_bytes=40 * MIB
        ),
        cost_estimate=pl.CostEstimate(
            flops=2 * devices * rows * columns * local,
            bytes_accessed=2 * columns * local,
            transcendentals=0,
        ),
        name="down",
    )(*arrays, *[codes] * SPLIT, scales)


def add_share(shares, stride):
    keep, send = shares
    return keep + exchange(send, stride).astype(jnp.float32)


def split_share(total):
    half = total.shape[0] // 2
    return total[:half], total[half:].astype(jnp.bfloat16)


def sum_over_devices(shares, strides):
    for stride in strides:
        total = add_share(shares, stride)
        shares = split_share(total)
    return total


def block_order(local, group):
    order = local // group
    while order > 32:
        order //= 2
    return order


def shards_piped(
    tokens, norm_gain, gate_codes, gate_scales, up_codes, up_scales, down_codes, down_scales
):
    devices = lax.axis_size(AXIS)
    width = tokens.shape[1]
    local = gate_codes.shape[1]
    group = down_codes.shape[0] // down_scales.shape[0]
    rows = tokens.shape[0] // 2
    table = np.kron(walsh(block_order(local, group)), hadamard_small())
    table = jnp.asarray(table.astype(ml_dtypes.bfloat16))

    grid = walsh(devices)
    both = np.stack(
        [[grid[me], [grid[me ^ k, me] for k in range(devices)]] for me in range(devices)]
    )
    signs = lax.dynamic_index_in_dim(
        jnp.asarray(both, jnp.float32), lax.axis_index(AXIS), 0, keepdims=False
    )
    weights = (gate_codes, gate_scales, up_codes, up_scales)

    half = width // 2
    near_far, far_near = [1, 4, 2], [4, 2, 1]
    left, right, own = norm(
        tokens,
        norm_gain,
        [(0, 0, rows, half), (0, half, rows, half), (rows, 0, rows, width)],
    )
    first = gather_doubling(left, near_far) + gather_doubling(right, far_near)
    near, straight = gather_flat_start(after(own, first[-1][0], first[devices - 1][0]), devices)

    arrays = gate_up(first, devices, rows, 1, *weights)
    hidden = swap_direct(arrays)
    near, straight = after((near, straight), arrays[1])
    second = gather_flat_end(near, straight)
    later_arrays = gate_up(second, devices, rows, 1, *weights)
    later_hidden = swap_direct(later_arrays)

    layout = single_layout(devices)
    hidden = all_after(hidden, later_arrays[1])
    arrays = rotate(hidden, layout, rows, signs, table)
    rotated = swap_direct(arrays)
    later_hidden = all_after(later_hidden, arrays[1])
    later_arrays = rotate(later_hidden, layout, rows, signs, table)
    later_rotated = swap_direct(later_arrays)
    rotated = all_after(rotated, later_arrays[1])

    def contract(pieces, strides, first_column, columns):
        return down(pieces, rows, strides, first_column, columns, down_codes, down_scales)

    order, other = [1, 2, 4], [2, 1, 4]
    above = split_share(add_share(contract(rotated, order, 0, width), order[0]))
    left = contract(all_after(later_rotated, above[1]), order, 0, half)
    above = split_share(add_share((above[0], above[1]), order[1]))
    right = contract(all_after(later_rotated, left[1], above[1]), other, half, half)
    above = add_share(above, order[2])
    for step in range(len(order)):
        left_total = add_share(left, order[step])
        right_total = add_share((right[0], after(right[1], left_total)), other[step])
        left, right = split_share(left_total), split_share(right_total)
    below = jnp.concatenate([left_total, right_total], axis=1)
    total = jnp.concatenate([above, below], axis=0)
    return (tokens.astype(jnp.float32) + total).astype(jnp.bfloat16)


def dequantize(codes, scales):
    blocks = scales.shape[0]
    height, width = codes.shape
    spread = codes.astype(jnp.float32).reshape(blocks, height // blocks, width) * scales[:, None, :]
    return spread.reshape(height, width).astype(jnp.bfloat16)


def shards_plain(
    tokens, norm_gain, gate_codes, gate_scales, up_codes, up_scales, down_codes, down_scales
):
    floated = tokens.astype(jnp.float32)
    normed = (
        floated
        * lax.rsqrt(jnp.mean(floated * floated, axis=1, keepdims=True) + EPSILON)
        * norm_gain
    ).astype(jnp.bfloat16)
    gate_weight = dequantize(gate_codes, gate_scales)
    up_weight = dequantize(up_codes, up_scales)
    down_weight = dequantize(down_codes, down_scales)
    piece = lax.all_gather(normed, AXIS, axis=0, tiled=True)
    gate = jnp.dot(piece, gate_weight, preferred_element_type=jnp.float32)
    upward = jnp.dot(piece, up_weight, preferred_element_type=jnp.float32)
    hidden = (jax.nn.silu(gate) * upward).astype(jnp.bfloat16)
    total_rows, local_width = hidden.shape
    devices = lax.axis_size(AXIS)
    local_walsh = down_scales.shape[0]
    group = down_codes.shape[0] // local_walsh
    blocks = hidden.astype(jnp.float32).reshape(total_rows, local_walsh, group)
    small_table = jnp.asarray(hadamard_small(), jnp.float32)
    local_table = jnp.asarray(walsh(local_walsh), jnp.float32)
    blocks = jnp.einsum("tia,ac->tic", blocks, small_table, precision=lax.Precision.HIGHEST)
    blocks = jnp.einsum("ji,tic->tjc", local_table, blocks, precision=lax.Precision.HIGHEST)
    blocks = blocks.reshape(total_rows, local_width)
    position = lax.axis_index(AXIS)
    for level in range(devices.bit_length() - 1):
        partner = exchange(blocks.astype(jnp.bfloat16), 1 << level).astype(blocks.dtype)
        signed = (1 - 2 * (position >> level & 1)).astype(jnp.float32)
        blocks = partner + signed * blocks
    rotated = (blocks * (devices * local_width) ** (-0.5)).astype(jnp.bfloat16)
    summed = lax.psum_scatter(
        jnp.dot(rotated, down_weight, preferred_element_type=jnp.float32),
        AXIS,
        scatter_dimension=0,
        tiled=True,
    )
    return (floated + summed).astype(jnp.bfloat16)


def shards(tokens, norm_gain, gate_codes, *others):
    devices = lax.axis_size(AXIS)
    rows, width = tokens.shape
    local = gate_codes.shape[1]
    if devices == 8 and rows % 32 == 0 and local % 896 == 0 and width % 1024 == 0:
        return shards_piped(tokens, norm_gain, gate_codes, *others)
    return shards_plain(tokens, norm_gain, gate_codes, *others)


def solution(mesh):
    return jax.shard_map(
        shards,
        mesh=mesh,
        in_specs=(
            P(("groups", "tensor", "dp"), None),
            P(),
            P(None, "tensor"),
            P(None, "tensor"),
            P(None, "tensor"),
            P(None, "tensor"),
            P("tensor", None),
            P("tensor", None),
        ),
        out_specs=P(("groups", "tensor", "dp"), None),
        check_vma=False,
    )
```

```python
import functools
import math

import jax
import jax.numpy as jnp
import ml_dtypes
import numpy as np
from jax import lax
from jax.experimental import pallas as pl
from jax.experimental.pallas import tpu as pltpu
from jax.sharding import PartitionSpec as P

EPSILON = 1e-05
AXIS = "tensor"
MIB = 1 << 20


def hadamard_small():
    modulus = 13
    residues = [number * number % modulus for number in range(1, modulus)]
    legendre = [0] + [1 if number in residues else -1 for number in range(1, modulus)]
    conference = np.zeros((modulus + 1, modulus + 1), np.int64)
    conference[0, 1:] = 1
    conference[1:, 0] = 1
    for row in range(1, modulus + 1):
        for column in range(1, modulus + 1):
            conference[row, column] = legendre[(column - row) % modulus]
    plus_block = np.array([[1, 1], [1, -1]])
    zero_block = np.array([[1, -1], [-1, -1]])
    return np.kron(conference, plus_block) + np.kron(np.eye(modulus + 1, dtype=np.int64), zero_block)


def walsh(order):
    table = np.ones((1, 1), np.int64)
    while table.shape[0] < order:
        table = np.kron(np.array([[1, 1], [1, -1]]), table)
    return table


def exchange(value, stride):
    return lax.ppermute(value, AXIS, [(i, i ^ stride) for i in range(lax.axis_size(AXIS))])


def after(value, *earlier):
    return lax.optimization_barrier((value, earlier))[0]


def swap_direct(arrays):
    out = list(arrays)
    for k in range(1, len(arrays)):
        out[k] = exchange(arrays[k], k)
    return [(array, 0) for array in out]


def all_after(pieces, *earlier):
    arrays, places = distinct(pieces)
    arrays = after(arrays, *earlier)
    return [(arrays[at], start) for at, start in places]


def distinct(pieces):
    arrays = []
    for array, _ in pieces:
        if not any(other is array for other in arrays):
            arrays.append(array)
    index = {id(array): at for at, array in enumerate(arrays)}
    return arrays, [(index[id(array)], start) for array, start in pieces]


SPLIT = 2


def split_blocks(height, tile, skip):
    return [
        pl.BlockSpec((height // SPLIT, tile), functools.partial(lambda part, i: (part, i + skip), part))
        for part in range(SPLIT)
    ]


def whole_blocks(arrays):
    return [pl.BlockSpec(array.shape, lambda i: (0, 0)) for array in arrays]


def norm_kernel(cuts, tokens_ref, gain_ref, *out_refs):
    floated = tokens_ref[...].astype(jnp.float32)
    inverse = lax.rsqrt(jnp.mean(floated * floated, axis=1, keepdims=True) + EPSILON)
    normed = (floated * inverse * gain_ref[...]).astype(jnp.bfloat16)
    for (row, column), out_ref in zip(cuts, out_refs):
        rows, columns = out_ref.shape
        out_ref[...] = normed[row : row + rows, column : column + columns]


def norm(tokens, gain, cuts):
    rows, width = tokens.shape
    return pl.pallas_call(
        functools.partial(norm_kernel, [cut[:2] for cut in cuts]),
        out_shape=[jax.ShapeDtypeStruct(cut[2:], jnp.bfloat16) for cut in cuts],
        compiler_params=pltpu.CompilerParams(vmem_limit_bytes=16 * MIB),
        cost_estimate=pl.CostEstimate(
            flops=5 * rows * width, bytes_accessed=4 * rows * width, transcendentals=rows
        ),
        name="norm",
    )(tokens, gain.reshape(1, width))


def gate_up_kernel(devices, rows, depth, qblock, me_ref, rows_ref, *refs):
    code_refs = refs[: 2 * SPLIT]
    gate_scale_ref, up_scale_ref = refs[2 * SPLIT : 2 * SPLIT + 2]
    out_refs = refs[2 * SPLIT + 2 : -1]
    held = refs[-1]
    span = code_refs[0].shape[0]

    @pl.when(pl.program_id(0) == 0)
    def _():
        for k in range(devices):
            start = pl.multiple_of((me_ref[0] ^ k) * rows, rows)
            held[k * rows : (k + 1) * rows, :] = rows_ref[pl.ds(start, rows), :]

    def weight(refs_of_codes, scales, at):
        parts = []
        for row in range(at, at + depth, qblock):
            codes = refs_of_codes[row // span][row % span : row % span + qblock, :]
            step = scales[row // qblock : row // qblock + 1, :]
            parts.append((codes.astype(jnp.float32) * step).astype(jnp.bfloat16))
        return jnp.concatenate(parts, axis=0)

    gate = up = None
    for at in range(0, SPLIT * span, depth):
        left = held[:, at : at + depth]
        right = weight(code_refs[:SPLIT], gate_scale_ref, at)
        term = jnp.dot(left, right, preferred_element_type=jnp.float32)
        gate = term if gate is None else gate + term
        right = weight(code_refs[SPLIT:], up_scale_ref, at)
        term = jnp.dot(left, right, preferred_element_type=jnp.float32)
        up = term if up is None else up + term
    hidden = (gate / (1.0 + jnp.exp(-gate)) * up).astype(jnp.bfloat16)
    for k, out_ref in enumerate(out_refs):
        out_ref[...] = hidden[k * rows : (k + 1) * rows]


def gate_up(me, gathered, devices, gate_codes, gate_scales, up_codes, up_scales):
    rows = gathered.shape[0] // devices
    width, local = gate_codes.shape
    blocks = gate_scales.shape[0]
    tile = 256
    codes = split_blocks(width, tile, 0)
    scales = pl.BlockSpec((blocks, tile), lambda i: (0, i))
    return pl.pallas_call(
        functools.partial(
            gate_up_kernel, devices, rows, 512, width // blocks
        ),
        grid=(local // tile,),
        in_specs=[pl.BlockSpec(memory_space=pltpu.SMEM)]
        + whole_blocks([gathered])
        + codes
        + codes
        + [scales, scales],
        out_specs=[pl.BlockSpec((rows, tile), lambda i: (0, i))] * devices,
        out_shape=[jax.ShapeDtypeStruct((rows, local), jnp.bfloat16)] * devices,
        scratch_shapes=[pltpu.VMEM((devices * rows, width), jnp.bfloat16)],
        compiler_params=pltpu.CompilerParams(
            dimension_semantics=("arbitrary",), vmem_limit_bytes=40 * MIB
        ),
        cost_estimate=pl.CostEstimate(
            flops=4 * devices * rows * width * local,
            bytes_accessed=4 * width * local,
            transcendentals=devices * rows * local,
        ),
        name="gate_up",
    )(me, gathered, *[gate_codes] * SPLIT, *[up_codes] * SPLIT, gate_scales, up_scales)


def rotate_kernel(places, rows, factor, ins, sign_ref, *refs):
    devices = len(places)
    piece_refs = refs[:ins]
    table_ref = refs[ins]
    out_refs = refs[ins + 1 : -1]
    held = refs[-1]
    local = piece_refs[0].shape[1]
    block = table_ref.shape[0]
    inner = local // block
    count = devices * inner
    for k, (source, start) in enumerate(places):
        sign = sign_ref[0, k].astype(jnp.bfloat16)
        for q in range(inner):
            at = (k * inner + q) * rows
            held[at : at + rows, :] = (
                piece_refs[source][start : start + rows, q * block : (q + 1) * block] * sign
            )
    for start in range(0, block, 256):
        stop = min(start + 256, block)
        product = jnp.dot(
            held[...], table_ref[:, start:stop], preferred_element_type=jnp.float32
        )
        values = [product[index * rows : (index + 1) * rows] for index in range(count)]
        stride = 1
        while stride < count:
            values = [
                values[index] + values[index ^ stride]
                if not index & stride
                else values[index ^ stride] - values[index]
                for index in range(count)
            ]
            stride *= 2
        for k in range(devices):
            scale = sign_ref[1, k] * factor
            for q in range(inner):
                out_refs[k][:, q * block + start : q * block + stop] = (
                    values[k * inner + q] * scale
                ).astype(jnp.bfloat16)


def rotate(pieces, rows, signs, table):
    devices = len(pieces)
    arrays, places = distinct(pieces)
    local = arrays[0].shape[1]
    block = table.shape[0]
    vmem = pl.BlockSpec(memory_space=pltpu.VMEM)
    return pl.pallas_call(
        functools.partial(
            rotate_kernel, places, rows, (devices * local) ** (-0.5), len(arrays)
        ),
        in_specs=[pl.BlockSpec(memory_space=pltpu.SMEM)] + [vmem] * (len(arrays) + 1),
        out_specs=[vmem] * devices,
        out_shape=[jax.ShapeDtypeStruct((rows, local), jnp.bfloat16)] * devices,
        scratch_shapes=[pltpu.VMEM((devices * rows * local // block, block), jnp.bfloat16)],
        compiler_params=pltpu.CompilerParams(vmem_limit_bytes=40 * MIB),
        cost_estimate=pl.CostEstimate(
            flops=2 * devices * rows * local * block,
            bytes_accessed=4 * devices * rows * local,
            transcendentals=devices * rows * local,
        ),
        name="rotate",
    )(signs, *arrays, table)


def down_kernel(places, rows, group, ins, me_ref, *refs):
    devices = len(places)
    piece_refs = refs[:ins]
    code_refs = refs[ins : ins + SPLIT]
    scale_ref, out_ref, held, weight = refs[ins + SPLIT :]

    @pl.when(pl.program_id(0) == 0)
    def _():
        for k in range(devices):
            at, start = places[k]
            into = pl.multiple_of((me_ref[0] ^ k) * rows, rows)
            held[pl.ds(into, rows), :] = piece_refs[at][start : start + rows, :]

    depth, tile = code_refs[0].shape
    repeat = math.lcm(group, 16)
    low_rows = lax.broadcasted_iota(jnp.int32, (8, tile), 0)
    total = None
    for part in range(SPLIT):
        for at in range(part * depth, (part + 1) * depth, repeat):
            steps = []
            for row in range(at, at + repeat, 8):
                first, last = row // group, (row + 7) // group
                step = jnp.broadcast_to(scale_ref[first : first + 1, :], (8, tile))
                if last != first:
                    other = jnp.broadcast_to(scale_ref[last : last + 1, :], (8, tile))
                    step = jnp.where(low_rows < last * group - row, step, other)
                steps.append(step)
            low = at - part * depth
            codes = code_refs[part][low : low + repeat, :].astype(jnp.float32)
            weight[at : at + repeat, :] = (codes * jnp.concatenate(steps, axis=0)).astype(
                jnp.bfloat16
            )
        term = jnp.dot(
            held[:, part * depth : (part + 1) * depth],
            weight[part * depth : (part + 1) * depth, :],
            preferred_element_type=jnp.float32,
        )
        total = term if total is None else total + term
    out_ref[...] = total.astype(jnp.bfloat16)


def down(me, pieces, rows, first_column, columns, codes, scales):
    devices = len(pieces)
    arrays, places = distinct(pieces)
    local = codes.shape[0]
    blocks = scales.shape[0]
    tile = 512
    skip = first_column // tile
    return pl.pallas_call(
        functools.partial(down_kernel, places, rows, local // blocks, len(arrays)),
        grid=(columns // tile,),
        in_specs=[pl.BlockSpec(memory_space=pltpu.SMEM)]
        + whole_blocks(arrays)
        + split_blocks(local, tile, skip)
        + [pl.BlockSpec((blocks, tile), lambda i: (0, i + skip))],
        out_specs=pl.BlockSpec((devices * rows, tile), lambda i: (0, i)),
        out_shape=jax.ShapeDtypeStruct((devices * rows, columns), jnp.bfloat16),
        scratch_shapes=[
            pltpu.VMEM((devices * rows, local), jnp.bfloat16),
            pltpu.VMEM((local, tile), jnp.bfloat16),
        ],
        compiler_params=pltpu.CompilerParams(
            dimension_semantics=("arbitrary",), vmem_limit_bytes=40 * MIB
        ),
        cost_estimate=pl.CostEstimate(
            flops=2 * devices * rows * columns * local,
            bytes_accessed=2 * columns * local,
            transcendentals=0,
        ),
        name="down",
    )(me, *arrays, *[codes] * SPLIT, scales)


def block_order(local, group):
    order = local // group
    while order > 32:
        order //= 2
    return order


def shards_piped(
    tokens, norm_gain, gate_codes, gate_scales, up_codes, up_scales, down_codes, down_scales
):
    devices = lax.axis_size(AXIS)
    width = tokens.shape[1]
    local = gate_codes.shape[1]
    group = down_codes.shape[0] // down_scales.shape[0]
    rows = tokens.shape[0] // 2
    table = np.kron(walsh(block_order(local, group)), hadamard_small())
    table = jnp.asarray(table.astype(ml_dtypes.bfloat16))

    grid = walsh(devices)
    both = np.stack(
        [[grid[me], [grid[me ^ k, me] for k in range(devices)]] for me in range(devices)]
    )
    signs = lax.dynamic_index_in_dim(
        jnp.asarray(both, jnp.float32), lax.axis_index(AXIS), 0, keepdims=False
    )
    weights = (gate_codes, gate_scales, up_codes, up_scales)

    me = lax.axis_index(AXIS).reshape(1)
    half = width // 2
    own = norm(tokens, norm_gain, [(0, 0, rows, width), (rows, 0, rows, width)])
    first = lax.all_gather(own[0], AXIS, axis=0, tiled=True)
    second = lax.all_gather(after(own[1], first), AXIS, axis=0, tiled=True)

    arrays = gate_up(me, first, devices, *weights)
    hidden = swap_direct(arrays)
    later_arrays = gate_up(me, after(second, arrays[1]), devices, *weights)
    later_hidden = swap_direct(later_arrays)

    hidden = all_after(hidden, later_arrays[1])
    arrays = rotate(hidden, rows, signs, table)
    rotated = swap_direct(arrays)
    later_hidden = all_after(later_hidden, arrays[1])
    later_arrays = rotate(later_hidden, rows, signs, table)
    later_rotated = swap_direct(later_arrays)
    rotated = all_after(rotated, later_arrays[1])

    def contract(pieces, first_column, columns):
        return down(me, pieces, rows, first_column, columns, down_codes, down_scales)

    def scatter(shares):
        return lax.psum_scatter(shares, AXIS, scatter_dimension=0, tiled=True)

    shares = contract(rotated, 0, width)
    above = scatter(shares)
    left = contract(all_after(later_rotated, above), 0, half)
    right = contract(all_after(later_rotated, left), half, half)
    residual = tokens.astype(jnp.float32)

    def add(start, columns, sums):
        base = residual[start : start + rows, columns : columns + sums.shape[1]]
        return (base + sums.astype(jnp.float32)).astype(jnp.bfloat16)

    above = add(0, 0, above)
    left = add(rows, 0, scatter(left))
    right = add(rows, half, after(scatter(right), left))
    return jnp.concatenate([above, jnp.concatenate([left, right], axis=1)], axis=0)


def dequantize(codes, scales):
    blocks = scales.shape[0]
    height, width = codes.shape
    spread = codes.astype(jnp.float32).reshape(blocks, height // blocks, width) * scales[:, None, :]
    return spread.reshape(height, width).astype(jnp.bfloat16)


def shards_plain(
    tokens, norm_gain, gate_codes, gate_scales, up_codes, up_scales, down_codes, down_scales
):
    floated = tokens.astype(jnp.float32)
    normed = (
        floated
        * lax.rsqrt(jnp.mean(floated * floated, axis=1, keepdims=True) + EPSILON)
        * norm_gain
    ).astype(jnp.bfloat16)
    gate_weight = dequantize(gate_codes, gate_scales)
    up_weight = dequantize(up_codes, up_scales)
    down_weight = dequantize(down_codes, down_scales)
    piece = lax.all_gather(normed, AXIS, axis=0, tiled=True)
    gate = jnp.dot(piece, gate_weight, preferred_element_type=jnp.float32)
    upward = jnp.dot(piece, up_weight, preferred_element_type=jnp.float32)
    hidden = (jax.nn.silu(gate) * upward).astype(jnp.bfloat16)
    total_rows, local_width = hidden.shape
    devices = lax.axis_size(AXIS)
    local_walsh = down_scales.shape[0]
    group = down_codes.shape[0] // local_walsh
    blocks = hidden.astype(jnp.float32).reshape(total_rows, local_walsh, group)
    small_table = jnp.asarray(hadamard_small(), jnp.float32)
    local_table = jnp.asarray(walsh(local_walsh), jnp.float32)
    blocks = jnp.einsum("tia,ac->tic", blocks, small_table, precision=lax.Precision.HIGHEST)
    blocks = jnp.einsum("ji,tic->tjc", local_table, blocks, precision=lax.Precision.HIGHEST)
    blocks = blocks.reshape(total_rows, local_width)
    position = lax.axis_index(AXIS)
    for level in range(devices.bit_length() - 1):
        partner = exchange(blocks.astype(jnp.bfloat16), 1 << level).astype(blocks.dtype)
        signed = (1 - 2 * (position >> level & 1)).astype(jnp.float32)
        blocks = partner + signed * blocks
    rotated = (blocks * (devices * local_width) ** (-0.5)).astype(jnp.bfloat16)
    summed = lax.psum_scatter(
        jnp.dot(rotated, down_weight, preferred_element_type=jnp.float32),
        AXIS,
        scatter_dimension=0,
        tiled=True,
    )
    return (floated + summed).astype(jnp.bfloat16)


def shards(tokens, norm_gain, gate_codes, *others):
    devices = lax.axis_size(AXIS)
    rows, width = tokens.shape
    local = gate_codes.shape[1]
    if devices == 8 and rows % 32 == 0 and local % 896 == 0 and width % 1024 == 0:
        return shards_piped(tokens, norm_gain, gate_codes, *others)
    return shards_plain(tokens, norm_gain, gate_codes, *others)


def solution(mesh):
    return jax.shard_map(
        shards,
        mesh=mesh,
        in_specs=(
            P(("groups", "tensor", "dp"), None),
            P(),
            P(None, "tensor"),
            P(None, "tensor"),
            P(None, "tensor"),
            P(None, "tensor"),
            P("tensor", None),
            P("tensor", None),
        ),
        out_specs=P(("groups", "tensor", "dp"), None),
        check_vma=False,
    )
```

```python
import functools
import math

import jax
import jax.numpy as jnp
import ml_dtypes
import numpy as np
from jax import lax
from jax.experimental import pallas as pl
from jax.experimental.pallas import tpu as pltpu
from jax.sharding import PartitionSpec as P

EPSILON = 1e-05
AXIS = "tensor"
MIB = 1 << 20


def hadamard_small():
    modulus = 13
    residues = [number * number % modulus for number in range(1, modulus)]
    legendre = [0] + [1 if number in residues else -1 for number in range(1, modulus)]
    conference = np.zeros((modulus + 1, modulus + 1), np.int64)
    conference[0, 1:] = 1
    conference[1:, 0] = 1
    for row in range(1, modulus + 1):
        for column in range(1, modulus + 1):
            conference[row, column] = legendre[(column - row) % modulus]
    plus_block = np.array([[1, 1], [1, -1]])
    zero_block = np.array([[1, -1], [-1, -1]])
    return np.kron(conference, plus_block) + np.kron(np.eye(modulus + 1, dtype=np.int64), zero_block)


def walsh(order):
    table = np.ones((1, 1), np.int64)
    while table.shape[0] < order:
        table = np.kron(np.array([[1, 1], [1, -1]]), table)
    return table


def exchange(value, stride):
    return lax.ppermute(value, AXIS, [(i, i ^ stride) for i in range(lax.axis_size(AXIS))])


def after(value, *earlier):
    return lax.optimization_barrier((value, earlier))[0]


def gather_tree(own, devices):
    pieces = {0: own}
    for k in sorted(range(1, devices), key=lambda k: (bin(k).count("1"), -k)):
        low = k & -k
        pieces[k] = exchange(pieces[k ^ low], low)
    return [(pieces[k], 0) for k in range(devices)]


def far_first(devices):
    return sorted(range(devices), key=lambda k: (-(k & (devices // 2)), -(k & (devices // 4)), k & 1 == 0))


def swap_direct(arrays):
    out = {}
    for k, array in zip(far_first(len(arrays)), arrays):
        out[k] = (exchange(array, k) if k else array, 0)
    return [out[k] for k in range(len(arrays))]


def all_after(pieces, *earlier):
    arrays, places = distinct(pieces)
    arrays = after(arrays, *earlier)
    return [(arrays[at], start) for at, start in places]


def distinct(pieces):
    arrays = []
    for array, _ in [pieces[k] for k in far_first(len(pieces))]:
        if not any(other is array for other in arrays):
            arrays.append(array)
    index = {id(array): at for at, array in enumerate(arrays)}
    return arrays, [(index[id(array)], start) for array, start in pieces]


SPLIT = 2


def split_blocks(height, tile, skip):
    return [
        pl.BlockSpec((height // SPLIT, tile), functools.partial(lambda part, i: (part, i + skip), part))
        for part in range(SPLIT)
    ]


def whole_blocks(arrays):
    return [pl.BlockSpec(array.shape, lambda i: (0, 0)) for array in arrays]


def norm_kernel(cuts, tokens_ref, gain_ref, *out_refs):
    floated = tokens_ref[...].astype(jnp.float32)
    inverse = lax.rsqrt(jnp.mean(floated * floated, axis=1, keepdims=True) + EPSILON)
    normed = (floated * inverse * gain_ref[...]).astype(jnp.bfloat16)
    for (row, column), out_ref in zip(cuts, out_refs):
        rows, columns = out_ref.shape
        out_ref[...] = normed[row : row + rows, column : column + columns]


def norm(tokens, gain, cuts):
    rows, width = tokens.shape
    return pl.pallas_call(
        functools.partial(norm_kernel, [cut[:2] for cut in cuts]),
        out_shape=[jax.ShapeDtypeStruct(cut[2:], jnp.bfloat16) for cut in cuts],
        compiler_params=pltpu.CompilerParams(vmem_limit_bytes=16 * MIB),
        cost_estimate=pl.CostEstimate(
            flops=5 * rows * width, bytes_accessed=4 * rows * width, transcendentals=rows
        ),
        name="norm",
    )(tokens, gain.reshape(1, width))


def gate_up_kernel(places, devices, rows, depth, qblock, ins, *refs):
    piece_refs = refs[:ins]
    code_refs = refs[ins : ins + 2 * SPLIT]
    gate_scale_ref, up_scale_ref = refs[ins + 2 * SPLIT : ins + 2 * SPLIT + 2]
    out_refs = refs[ins + 2 * SPLIT + 2 : -1]
    held = refs[-1]
    span = code_refs[0].shape[0]

    @pl.when(pl.program_id(0) == 0)
    def _():
        for k, (at, start) in enumerate(places):
            held[k * rows : (k + 1) * rows, :] = piece_refs[at][start : start + rows, :]

    def weight(refs_of_codes, scales, at):
        parts = []
        for row in range(at, at + depth, qblock):
            codes = refs_of_codes[row // span][row % span : row % span + qblock, :]
            step = scales[row // qblock : row // qblock + 1, :]
            parts.append((codes.astype(jnp.float32) * step).astype(jnp.bfloat16))
        return jnp.concatenate(parts, axis=0)

    gate = up = None
    for at in range(0, SPLIT * span, depth):
        left = held[:, at : at + depth]
        right = weight(code_refs[:SPLIT], gate_scale_ref, at)
        term = jnp.dot(left, right, preferred_element_type=jnp.float32)
        gate = term if gate is None else gate + term
        right = weight(code_refs[SPLIT:], up_scale_ref, at)
        term = jnp.dot(left, right, preferred_element_type=jnp.float32)
        up = term if up is None else up + term
    hidden = (gate / (1.0 + jnp.exp(-gate)) * up).astype(jnp.bfloat16)
    for k, out_ref in zip(far_first(devices), out_refs):
        out_ref[...] = hidden[k * rows : (k + 1) * rows]


def gate_up(pieces, rows, gate_codes, gate_scales, up_codes, up_scales):
    devices = len(pieces)
    arrays, places = distinct(pieces)
    width, local = gate_codes.shape
    blocks = gate_scales.shape[0]
    tile = 256
    codes = split_blocks(width, tile, 0)
    scales = pl.BlockSpec((blocks, tile), lambda i: (0, i))
    return pl.pallas_call(
        functools.partial(
            gate_up_kernel, places, devices, rows, 512, width // blocks, len(arrays)
        ),
        grid=(local // tile,),
        in_specs=whole_blocks(arrays) + codes + codes + [scales, scales],
        out_specs=[pl.BlockSpec((rows, tile), lambda i: (0, i))] * devices,
        out_shape=[jax.ShapeDtypeStruct((rows, local), jnp.bfloat16)] * devices,
        scratch_shapes=[pltpu.VMEM((devices * rows, width), jnp.bfloat16)],
        compiler_params=pltpu.CompilerParams(
            dimension_semantics=("arbitrary",), vmem_limit_bytes=40 * MIB
        ),
        cost_estimate=pl.CostEstimate(
            flops=4 * devices * rows * width * local,
            bytes_accessed=4 * width * local,
            transcendentals=devices * rows * local,
        ),
        name="gate_up",
    )(*arrays, *[gate_codes] * SPLIT, *[up_codes] * SPLIT, gate_scales, up_scales)


def rotate_kernel(places, rows, factor, ins, sign_ref, *refs):
    devices = len(places)
    piece_refs = refs[:ins]
    table_ref = refs[ins]
    out_refs = dict(zip(far_first(devices), refs[ins + 1 : -1]))
    held = refs[-1]
    local = piece_refs[0].shape[1]
    block = table_ref.shape[0]
    inner = local // block
    count = devices * inner
    for k, (source, start) in enumerate(places):
        sign = sign_ref[0, k].astype(jnp.bfloat16)
        for q in range(inner):
            at = (k * inner + q) * rows
            held[at : at + rows, :] = (
                piece_refs[source][start : start + rows, q * block : (q + 1) * block] * sign
            )
    for start in range(0, block, 256):
        stop = min(start + 256, block)
        product = jnp.dot(
            held[...], table_ref[:, start:stop], preferred_element_type=jnp.float32
        )
        values = [product[index * rows : (index + 1) * rows] for index in range(count)]
        stride = 1
        while stride < count:
            values = [
                values[index] + values[index ^ stride]
                if not index & stride
                else values[index ^ stride] - values[index]
                for index in range(count)
            ]
            stride *= 2
        for k in range(devices):
            scale = sign_ref[1, k] * factor
            for q in range(inner):
                out_refs[k][:, q * block + start : q * block + stop] = (
                    values[k * inner + q] * scale
                ).astype(jnp.bfloat16)


def rotate(pieces, rows, signs, table):
    devices = len(pieces)
    arrays, places = distinct(pieces)
    local = arrays[0].shape[1]
    block = table.shape[0]
    vmem = pl.BlockSpec(memory_space=pltpu.VMEM)
    return pl.pallas_call(
        functools.partial(
            rotate_kernel, places, rows, (devices * local) ** (-0.5), len(arrays)
        ),
        in_specs=[pl.BlockSpec(memory_space=pltpu.SMEM)] + [vmem] * (len(arrays) + 1),
        out_specs=[vmem] * devices,
        out_shape=[jax.ShapeDtypeStruct((rows, local), jnp.bfloat16)] * devices,
        scratch_shapes=[pltpu.VMEM((devices * rows * local // block, block), jnp.bfloat16)],
        compiler_params=pltpu.CompilerParams(vmem_limit_bytes=40 * MIB),
        cost_estimate=pl.CostEstimate(
            flops=2 * devices * rows * local * block,
            bytes_accessed=4 * devices * rows * local,
            transcendentals=devices * rows * local,
        ),
        name="rotate",
    )(signs, *arrays, table)


def down_kernel(places, rows, group, order, ins, *refs):
    devices = len(places)
    piece_refs = refs[:ins]
    code_refs = refs[ins : ins + SPLIT]
    scale_ref, keep_ref, send_ref, held, weight = refs[ins + SPLIT :]
    half = devices // 2

    @pl.when(pl.program_id(0) == 0)
    def _():
        for place, k in enumerate(order):
            at, start = places[k]
            held[place * rows : (place + 1) * rows, :] = piece_refs[at][start : start + rows, :]

    depth, tile = code_refs[0].shape
    repeat = math.lcm(group, 16)
    low_rows = lax.broadcasted_iota(jnp.int32, (8, tile), 0)
    total = None
    for part in range(SPLIT):
        for at in range(part * depth, (part + 1) * depth, repeat):
            steps = []
            for row in range(at, at + repeat, 8):
                first, last = row // group, (row + 7) // group
                step = jnp.broadcast_to(scale_ref[first : first + 1, :], (8, tile))
                if last != first:
                    other = jnp.broadcast_to(scale_ref[last : last + 1, :], (8, tile))
                    step = jnp.where(low_rows < last * group - row, step, other)
                steps.append(step)
            low = at - part * depth
            codes = code_refs[part][low : low + repeat, :].astype(jnp.float32)
            weight[at : at + repeat, :] = (codes * jnp.concatenate(steps, axis=0)).astype(
                jnp.bfloat16
            )
        term = jnp.dot(
            held[:, part * depth : (part + 1) * depth],
            weight[part * depth : (part + 1) * depth, :],
            preferred_element_type=jnp.float32,
        )
        total = term if total is None else total + term
    keep_ref[...] = total[: half * rows]
    send_ref[...] = total[half * rows :].astype(jnp.bfloat16)


def down(pieces, rows, strides, first_column, columns, codes, scales):
    devices = len(pieces)
    arrays, places = distinct(pieces)
    local = codes.shape[0]
    blocks = scales.shape[0]
    tile = 512
    skip = first_column // tile
    levels = len(strides)
    order = sorted(
        range(devices),
        key=lambda k: sum(1 << (levels - 1 - i) for i, stride in enumerate(strides) if k & stride),
    )
    out_rows = devices // 2 * rows
    return pl.pallas_call(
        functools.partial(down_kernel, places, rows, local // blocks, order, len(arrays)),
        grid=(columns // tile,),
        in_specs=whole_blocks(arrays)
        + split_blocks(local, tile, skip)
        + [pl.BlockSpec((blocks, tile), lambda i: (0, i + skip))],
        out_specs=[pl.BlockSpec((out_rows, tile), lambda i: (0, i))] * 2,
        out_shape=[
            jax.ShapeDtypeStruct((out_rows, columns), jnp.float32),
            jax.ShapeDtypeStruct((out_rows, columns), jnp.bfloat16),
        ],
        scratch_shapes=[
            pltpu.VMEM((devices * rows, local), jnp.bfloat16),
            pltpu.VMEM((local, tile), jnp.bfloat16),
        ],
        compiler_params=pltpu.CompilerParams(
            dimension_semantics=("arbitrary",), vmem_limit_bytes=40 * MIB
        ),
        cost_estimate=pl.CostEstimate(
            flops=2 * devices * rows * columns * local,
            bytes_accessed=2 * columns * local,
            transcendentals=0,
        ),
        name="down",
    )(*arrays, *[codes] * SPLIT, scales)


def add_share(shares, stride, *earlier):
    keep, send = shares
    return keep + after(exchange(send, stride), *earlier).astype(jnp.float32)


def split_share(total):
    half = total.shape[0] // 2
    return total[:half], total[half:].astype(jnp.bfloat16)


def block_order(local, group):
    order = local // group
    while order > 32:
        order //= 2
    return order


def shards_piped(
    tokens, norm_gain, gate_codes, gate_scales, up_codes, up_scales, down_codes, down_scales
):
    devices = lax.axis_size(AXIS)
    width = tokens.shape[1]
    local = gate_codes.shape[1]
    group = down_codes.shape[0] // down_scales.shape[0]
    rows = tokens.shape[0] // 2
    table = np.kron(walsh(block_order(local, group)), hadamard_small())
    table = jnp.asarray(table.astype(ml_dtypes.bfloat16))

    grid = walsh(devices)
    both = np.stack(
        [[grid[me], [grid[me ^ k, me] for k in range(devices)]] for me in range(devices)]
    )
    signs = lax.dynamic_index_in_dim(
        jnp.asarray(both, jnp.float32), lax.axis_index(AXIS), 0, keepdims=False
    )
    weights = (gate_codes, gate_scales, up_codes, up_scales)

    half = width // 2
    own = norm(tokens, norm_gain, [(0, 0, rows, width), (rows, 0, rows, width)])
    first, second = [gather_tree(piece, devices) for piece in own]

    arrays = gate_up(first, rows, *weights)
    hidden = swap_direct(arrays)
    later_arrays = gate_up(all_after(second, arrays[0]), rows, *weights)
    later_hidden = swap_direct(later_arrays)

    arrays = rotate(all_after(hidden, later_arrays[0]), rows, signs, table)
    rotated = swap_direct(arrays)
    later_arrays = rotate(all_after(later_hidden, arrays[0]), rows, signs, table)
    later_rotated = swap_direct(later_arrays)

    def contract(pieces, strides, first_column, columns):
        return down(pieces, rows, strides, first_column, columns, down_codes, down_scales)

    order, other = [1, 2, 4], [2, 1, 4]
    rotated = all_after(rotated, later_arrays[0])
    top_left = contract(rotated, order, 0, half)
    top_right = contract(all_after(rotated, top_left[1]), other, half, half)
    left = contract(all_after(later_rotated, top_right[1]), order, 0, half)
    top_left = split_share(add_share(top_left, order[0], left[1]))
    top_right = split_share(add_share(top_right, other[0], left[1]))
    right = contract(
        all_after(later_rotated, left[1], top_left[1], top_right[1]), other, half, half
    )
    top_left = split_share(add_share(top_left, order[1], right[1]))
    top_right = split_share(add_share(top_right, other[1], right[1]))
    left = split_share(add_share(left, order[0], top_left[1], top_right[1]))
    right = split_share(add_share(right, other[0], left[1]))
    top_left = add_share(top_left, order[2], right[1])
    top_right = add_share(top_right, other[2], right[1])
    left = split_share(add_share(left, order[1], top_left, top_right))
    right = split_share(add_share(right, other[1], left[1]))
    left = add_share(left, order[2])
    right = add_share(right, other[2], left)
    above = jnp.concatenate([top_left, top_right], axis=1)
    below = jnp.concatenate([left, right], axis=1)
    total = jnp.concatenate([above, below], axis=0)
    return (tokens.astype(jnp.float32) + total).astype(jnp.bfloat16)


def dequantize(codes, scales):
    blocks = scales.shape[0]
    height, width = codes.shape
    spread = codes.astype(jnp.float32).reshape(blocks, height // blocks, width) * scales[:, None, :]
    return spread.reshape(height, width).astype(jnp.bfloat16)


def shards_plain(
    tokens, norm_gain, gate_codes, gate_scales, up_codes, up_scales, down_codes, down_scales
):
    floated = tokens.astype(jnp.float32)
    normed = (
        floated
        * lax.rsqrt(jnp.mean(floated * floated, axis=1, keepdims=True) + EPSILON)
        * norm_gain
    ).astype(jnp.bfloat16)
    gate_weight = dequantize(gate_codes, gate_scales)
    up_weight = dequantize(up_codes, up_scales)
    down_weight = dequantize(down_codes, down_scales)
    piece = lax.all_gather(normed, AXIS, axis=0, tiled=True)
    gate = jnp.dot(piece, gate_weight, preferred_element_type=jnp.float32)
    upward = jnp.dot(piece, up_weight, preferred_element_type=jnp.float32)
    hidden = (jax.nn.silu(gate) * upward).astype(jnp.bfloat16)
    total_rows, local_width = hidden.shape
    devices = lax.axis_size(AXIS)
    local_walsh = down_scales.shape[0]
    group = down_codes.shape[0] // local_walsh
    blocks = hidden.astype(jnp.float32).reshape(total_rows, local_walsh, group)
    small_table = jnp.asarray(hadamard_small(), jnp.float32)
    local_table = jnp.asarray(walsh(local_walsh), jnp.float32)
    blocks = jnp.einsum("tia,ac->tic", blocks, small_table, precision=lax.Precision.HIGHEST)
    blocks = jnp.einsum("ji,tic->tjc", local_table, blocks, precision=lax.Precision.HIGHEST)
    blocks = blocks.reshape(total_rows, local_width)
    position = lax.axis_index(AXIS)
    for level in range(devices.bit_length() - 1):
        partner = exchange(blocks.astype(jnp.bfloat16), 1 << level).astype(blocks.dtype)
        signed = (1 - 2 * (position >> level & 1)).astype(jnp.float32)
        blocks = partner + signed * blocks
    rotated = (blocks * (devices * local_width) ** (-0.5)).astype(jnp.bfloat16)
    summed = lax.psum_scatter(
        jnp.dot(rotated, down_weight, preferred_element_type=jnp.float32),
        AXIS,
        scatter_dimension=0,
        tiled=True,
    )
    return (floated + summed).astype(jnp.bfloat16)


def shards(tokens, norm_gain, gate_codes, *others):
    devices = lax.axis_size(AXIS)
    rows, width = tokens.shape
    local = gate_codes.shape[1]
    if devices == 8 and rows % 32 == 0 and local % 896 == 0 and width % 1024 == 0:
        return shards_piped(tokens, norm_gain, gate_codes, *others)
    return shards_plain(tokens, norm_gain, gate_codes, *others)


def solution(mesh):
    return jax.shard_map(
        shards,
        mesh=mesh,
        in_specs=(
            P(("groups", "tensor", "dp"), None),
            P(),
            P(None, "tensor"),
            P(None, "tensor"),
            P(None, "tensor"),
            P(None, "tensor"),
            P("tensor", None),
            P("tensor", None),
        ),
        out_specs=P(("groups", "tensor", "dp"), None),
        check_vma=False,
    )
```

```python
import functools
import math

import jax
import jax.numpy as jnp
import ml_dtypes
import numpy as np
from jax import lax
from jax.experimental import pallas as pl
from jax.experimental.pallas import tpu as pltpu
from jax.sharding import PartitionSpec as P

EPSILON = 1e-05
AXIS = "tensor"
MIB = 1 << 20


def hadamard_small():
    modulus = 13
    residues = [number * number % modulus for number in range(1, modulus)]
    legendre = [0] + [1 if number in residues else -1 for number in range(1, modulus)]
    conference = np.zeros((modulus + 1, modulus + 1), np.int64)
    conference[0, 1:] = 1
    conference[1:, 0] = 1
    for row in range(1, modulus + 1):
        for column in range(1, modulus + 1):
            conference[row, column] = legendre[(column - row) % modulus]
    plus_block = np.array([[1, 1], [1, -1]])
    zero_block = np.array([[1, -1], [-1, -1]])
    return np.kron(conference, plus_block) + np.kron(np.eye(modulus + 1, dtype=np.int64), zero_block)


def walsh(order):
    table = np.ones((1, 1), np.int64)
    while table.shape[0] < order:
        table = np.kron(np.array([[1, 1], [1, -1]]), table)
    return table


def exchange(value, stride):
    return lax.ppermute(value, AXIS, [(i, i ^ stride) for i in range(lax.axis_size(AXIS))])


def after(value, *earlier):
    return lax.optimization_barrier((value, earlier))[0]


def gather_tree(own, devices):
    pieces = {0: own}
    for k in sorted(range(1, devices), key=lambda k: (bin(k).count("1"), -k)):
        low = k & -k
        pieces[k] = exchange(pieces[k ^ low], low)
    return [(pieces[k], 0) for k in range(devices)]


def departure(devices):
    half = devices // 2
    return [1, 2] + list(range(devices - 1, half - 1, -1)) + list(range(3, half)) + [0]


def swap_direct(arrays):
    out = {}
    for k, array in zip(departure(len(arrays)), arrays):
        out[k] = (exchange(array, k) if k else array, 0)
    return [out[k] for k in range(len(arrays))]


def all_after(pieces, *earlier):
    arrays, places = distinct(pieces)
    arrays = after(arrays, *earlier)
    return [(arrays[at], start) for at, start in places]


def distinct(pieces):
    arrays = []
    for array, _ in [pieces[k] for k in departure(len(pieces))]:
        if not any(other is array for other in arrays):
            arrays.append(array)
    index = {id(array): at for at, array in enumerate(arrays)}
    return arrays, [(index[id(array)], start) for array, start in pieces]


SPLIT = 2


def split_blocks(height, tile, skip):
    return [
        pl.BlockSpec((height // SPLIT, tile), functools.partial(lambda part, i: (part, i + skip), part))
        for part in range(SPLIT)
    ]


def whole_blocks(arrays):
    return [pl.BlockSpec(array.shape, lambda i: (0, 0)) for array in arrays]


def norm_kernel(cuts, tokens_ref, gain_ref, *out_refs):
    floated = tokens_ref[...].astype(jnp.float32)
    inverse = lax.rsqrt(jnp.mean(floated * floated, axis=1, keepdims=True) + EPSILON)
    normed = (floated * inverse * gain_ref[...]).astype(jnp.bfloat16)
    for (row, column), out_ref in zip(cuts, out_refs):
        rows, columns = out_ref.shape
        out_ref[...] = normed[row : row + rows, column : column + columns]


def norm(tokens, gain, cuts):
    rows, width = tokens.shape
    return pl.pallas_call(
        functools.partial(norm_kernel, [cut[:2] for cut in cuts]),
        out_shape=[jax.ShapeDtypeStruct(cut[2:], jnp.bfloat16) for cut in cuts],
        compiler_params=pltpu.CompilerParams(vmem_limit_bytes=16 * MIB),
        cost_estimate=pl.CostEstimate(
            flops=5 * rows * width, bytes_accessed=4 * rows * width, transcendentals=rows
        ),
        name="norm",
    )(tokens, gain.reshape(1, width))


def gate_up_kernel(places, devices, rows, depth, qblock, ins, *refs):
    piece_refs = refs[:ins]
    code_refs = refs[ins : ins + 2 * SPLIT]
    gate_scale_ref, up_scale_ref = refs[ins + 2 * SPLIT : ins + 2 * SPLIT + 2]
    out_refs = refs[ins + 2 * SPLIT + 2 : -1]
    held = refs[-1]
    span = code_refs[0].shape[0]

    @pl.when(pl.program_id(0) == 0)
    def _():
        for k, (at, start) in enumerate(places):
            held[k * rows : (k + 1) * rows, :] = piece_refs[at][start : start + rows, :]

    def weight(refs_of_codes, scales, at):
        parts = []
        for row in range(at, at + depth, qblock):
            codes = refs_of_codes[row // span][row % span : row % span + qblock, :]
            step = scales[row // qblock : row // qblock + 1, :]
            parts.append((codes.astype(jnp.float32) * step).astype(jnp.bfloat16))
        return jnp.concatenate(parts, axis=0)

    gate = up = None
    for at in range(0, SPLIT * span, depth):
        left = held[:, at : at + depth]
        right = weight(code_refs[:SPLIT], gate_scale_ref, at)
        term = jnp.dot(left, right, preferred_element_type=jnp.float32)
        gate = term if gate is None else gate + term
        right = weight(code_refs[SPLIT:], up_scale_ref, at)
        term = jnp.dot(left, right, preferred_element_type=jnp.float32)
        up = term if up is None else up + term
    hidden = (gate / (1.0 + jnp.exp(-gate)) * up).astype(jnp.bfloat16)
    for k, out_ref in zip(departure(devices), out_refs):
        out_ref[...] = hidden[k * rows : (k + 1) * rows]


def gate_up(pieces, rows, gate_codes, gate_scales, up_codes, up_scales):
    devices = len(pieces)
    arrays, places = distinct(pieces)
    width, local = gate_codes.shape
    blocks = gate_scales.shape[0]
    tile = 256
    codes = split_blocks(width, tile, 0)
    scales = pl.BlockSpec((blocks, tile), lambda i: (0, i))
    return pl.pallas_call(
        functools.partial(
            gate_up_kernel, places, devices, rows, 512, width // blocks, len(arrays)
        ),
        grid=(local // tile,),
        in_specs=whole_blocks(arrays) + codes + codes + [scales, scales],
        out_specs=[pl.BlockSpec((rows, tile), lambda i: (0, i))] * devices,
        out_shape=[jax.ShapeDtypeStruct((rows, local), jnp.bfloat16)] * devices,
        scratch_shapes=[pltpu.VMEM((devices * rows, width), jnp.bfloat16)],
        compiler_params=pltpu.CompilerParams(
            dimension_semantics=("arbitrary",), vmem_limit_bytes=40 * MIB
        ),
        cost_estimate=pl.CostEstimate(
            flops=4 * devices * rows * width * local,
            bytes_accessed=4 * width * local,
            transcendentals=devices * rows * local,
        ),
        name="gate_up",
    )(*arrays, *[gate_codes] * SPLIT, *[up_codes] * SPLIT, gate_scales, up_scales)


def rotate_kernel(places, rows, factor, ins, sign_ref, *refs):
    devices = len(places)
    piece_refs = refs[:ins]
    table_ref = refs[ins]
    out_refs = dict(zip(departure(devices), refs[ins + 1 : -1]))
    held = refs[-1]
    local = piece_refs[0].shape[1]
    block = table_ref.shape[0]
    inner = local // block
    count = devices * inner
    for k, (source, start) in enumerate(places):
        sign = sign_ref[0, k].astype(jnp.bfloat16)
        for q in range(inner):
            at = (k * inner + q) * rows
            held[at : at + rows, :] = (
                piece_refs[source][start : start + rows, q * block : (q + 1) * block] * sign
            )
    for start in range(0, block, 256):
        stop = min(start + 256, block)
        product = jnp.dot(
            held[...], table_ref[:, start:stop], preferred_element_type=jnp.float32
        )
        values = [product[index * rows : (index + 1) * rows] for index in range(count)]
        stride = 1
        while stride < count:
            values = [
                values[index] + values[index ^ stride]
                if not index & stride
                else values[index ^ stride] - values[index]
                for index in range(count)
            ]
            stride *= 2
        for k in range(devices):
            scale = sign_ref[1, k] * factor
            for q in range(inner):
                out_refs[k][:, q * block + start : q * block + stop] = (
                    values[k * inner + q] * scale
                ).astype(jnp.bfloat16)


def rotate(pieces, rows, signs, table):
    devices = len(pieces)
    arrays, places = distinct(pieces)
    local = arrays[0].shape[1]
    block = table.shape[0]
    vmem = pl.BlockSpec(memory_space=pltpu.VMEM)
    return pl.pallas_call(
        functools.partial(
            rotate_kernel, places, rows, (devices * local) ** (-0.5), len(arrays)
        ),
        in_specs=[pl.BlockSpec(memory_space=pltpu.SMEM)] + [vmem] * (len(arrays) + 1),
        out_specs=[vmem] * devices,
        out_shape=[jax.ShapeDtypeStruct((rows, local), jnp.bfloat16)] * devices,
        scratch_shapes=[pltpu.VMEM((devices * rows * local // block, block), jnp.bfloat16)],
        compiler_params=pltpu.CompilerParams(vmem_limit_bytes=40 * MIB),
        cost_estimate=pl.CostEstimate(
            flops=2 * devices * rows * local * block,
            bytes_accessed=4 * devices * rows * local,
            transcendentals=devices * rows * local,
        ),
        name="rotate",
    )(signs, *arrays, table)


def down_kernel(places, rows, group, order, ins, *refs):
    devices = len(places)
    piece_refs = refs[:ins]
    code_refs = refs[ins : ins + SPLIT]
    scale_ref, keep_ref, send_ref, held, weight = refs[ins + SPLIT :]
    half = devices // 2

    @pl.when(pl.program_id(0) == 0)
    def _():
        for place, k in enumerate(order):
            at, start = places[k]
            held[place * rows : (place + 1) * rows, :] = piece_refs[at][start : start + rows, :]

    depth, tile = code_refs[0].shape
    repeat = math.lcm(group, 16)
    low_rows = lax.broadcasted_iota(jnp.int32, (8, tile), 0)
    total = None
    for part in range(SPLIT):
        for at in range(part * depth, (part + 1) * depth, repeat):
            steps = []
            for row in range(at, at + repeat, 8):
                first, last = row // group, (row + 7) // group
                step = jnp.broadcast_to(scale_ref[first : first + 1, :], (8, tile))
                if last != first:
                    other = jnp.broadcast_to(scale_ref[last : last + 1, :], (8, tile))
                    step = jnp.where(low_rows < last * group - row, step, other)
                steps.append(step)
            low = at - part * depth
            codes = code_refs[part][low : low + repeat, :].astype(jnp.float32)
            weight[at : at + repeat, :] = (codes * jnp.concatenate(steps, axis=0)).astype(
                jnp.bfloat16
            )
        term = jnp.dot(
            held[:, part * depth : (part + 1) * depth],
            weight[part * depth : (part + 1) * depth, :],
            preferred_element_type=jnp.float32,
        )
        total = term if total is None else total + term
    keep_ref[...] = total[: half * rows]
    send_ref[...] = total[half * rows :].astype(jnp.bfloat16)


def down(pieces, rows, strides, first_column, columns, codes, scales):
    devices = len(pieces)
    arrays, places = distinct(pieces)
    local = codes.shape[0]
    blocks = scales.shape[0]
    tile = 512
    skip = first_column // tile
    levels = len(strides)
    order = sorted(
        range(devices),
        key=lambda k: sum(1 << (levels - 1 - i) for i, stride in enumerate(strides) if k & stride),
    )
    out_rows = devices // 2 * rows
    return pl.pallas_call(
        functools.partial(down_kernel, places, rows, local // blocks, order, len(arrays)),
        grid=(columns // tile,),
        in_specs=whole_blocks(arrays)
        + split_blocks(local, tile, skip)
        + [pl.BlockSpec((blocks, tile), lambda i: (0, i + skip))],
        out_specs=[pl.BlockSpec((out_rows, tile), lambda i: (0, i))] * 2,
        out_shape=[
            jax.ShapeDtypeStruct((out_rows, columns), jnp.float32),
            jax.ShapeDtypeStruct((out_rows, columns), jnp.bfloat16),
        ],
        scratch_shapes=[
            pltpu.VMEM((devices * rows, local), jnp.bfloat16),
            pltpu.VMEM((local, tile), jnp.bfloat16),
        ],
        compiler_params=pltpu.CompilerParams(
            dimension_semantics=("arbitrary",), vmem_limit_bytes=40 * MIB
        ),
        cost_estimate=pl.CostEstimate(
            flops=2 * devices * rows * columns * local,
            bytes_accessed=2 * columns * local,
            transcendentals=0,
        ),
        name="down",
    )(*arrays, *[codes] * SPLIT, scales)


def add_share(shares, stride, *earlier):
    keep, send = shares
    return keep + after(exchange(send, stride), *earlier).astype(jnp.float32)


def split_share(total):
    half = total.shape[0] // 2
    return total[:half], total[half:].astype(jnp.bfloat16)


def block_order(local, group):
    order = local // group
    while order > 32:
        order //= 2
    return order


def shards_piped(
    tokens, norm_gain, gate_codes, gate_scales, up_codes, up_scales, down_codes, down_scales
):
    devices = lax.axis_size(AXIS)
    width = tokens.shape[1]
    local = gate_codes.shape[1]
    group = down_codes.shape[0] // down_scales.shape[0]
    rows = tokens.shape[0] // 2
    table = np.kron(walsh(block_order(local, group)), hadamard_small())
    table = jnp.asarray(table.astype(ml_dtypes.bfloat16))

    grid = walsh(devices)
    both = np.stack(
        [[grid[me], [grid[me ^ k, me] for k in range(devices)]] for me in range(devices)]
    )
    signs = lax.dynamic_index_in_dim(
        jnp.asarray(both, jnp.float32), lax.axis_index(AXIS), 0, keepdims=False
    )
    weights = (gate_codes, gate_scales, up_codes, up_scales)

    half = width // 2
    most = max(half, width // 512 * 5 // 8 * 512)
    own = norm(tokens, norm_gain, [(0, 0, rows, width), (rows, 0, rows, width)])
    first, second = [gather_tree(piece, devices) for piece in own]

    arrays = gate_up(first, rows, *weights)
    hidden = swap_direct(arrays)
    later_arrays = gate_up(all_after(second, arrays[-1]), rows, *weights)
    later_hidden = swap_direct(later_arrays)

    arrays = rotate(all_after(hidden, later_arrays[-1]), rows, signs, table)
    rotated = swap_direct(arrays)
    later_arrays = rotate(all_after(later_hidden, arrays[-1]), rows, signs, table)
    later_rotated = swap_direct(later_arrays)

    def contract(pieces, strides, first_column, columns):
        return down(pieces, rows, strides, first_column, columns, down_codes, down_scales)

    order, other = [1, 2, 4], [2, 1, 4]
    rotated = all_after(rotated, later_arrays[-1])
    top_left = contract(rotated, order, 0, half)
    top_right = contract(all_after(rotated, top_left[1]), other, half, half)
    left = contract(all_after(later_rotated, top_right[1]), order, 0, most)
    top_left = split_share(add_share(top_left, order[0], left[1]))
    top_right = split_share(add_share(top_right, other[0], left[1]))
    right = contract(
        all_after(later_rotated, left[1], top_left[1], top_right[1]), other, most, width - most
    )
    top_left = split_share(add_share(top_left, order[1], right[1]))
    top_right = split_share(add_share(top_right, other[1], right[1]))
    left = split_share(add_share(left, order[0], top_left[1], top_right[1]))
    right = split_share(add_share(right, other[0], left[1]))
    top_left = add_share(top_left, order[2], right[1])
    top_right = add_share(top_right, other[2], right[1])
    left = split_share(add_share(left, order[1], top_left, top_right))
    right = split_share(add_share(right, other[1], left[1]))
    left = add_share(left, order[2])
    right = add_share(right, other[2], left)
    above = jnp.concatenate([top_left, top_right], axis=1)
    below = jnp.concatenate([left, right], axis=1)
    total = jnp.concatenate([above, below], axis=0)
    return (tokens.astype(jnp.float32) + total).astype(jnp.bfloat16)


def dequantize(codes, scales):
    blocks = scales.shape[0]
    height, width = codes.shape
    spread = codes.astype(jnp.float32).reshape(blocks, height // blocks, width) * scales[:, None, :]
    return spread.reshape(height, width).astype(jnp.bfloat16)


def shards_plain(
    tokens, norm_gain, gate_codes, gate_scales, up_codes, up_scales, down_codes, down_scales
):
    floated = tokens.astype(jnp.float32)
    normed = (
        floated
        * lax.rsqrt(jnp.mean(floated * floated, axis=1, keepdims=True) + EPSILON)
        * norm_gain
    ).astype(jnp.bfloat16)
    gate_weight = dequantize(gate_codes, gate_scales)
    up_weight = dequantize(up_codes, up_scales)
    down_weight = dequantize(down_codes, down_scales)
    piece = lax.all_gather(normed, AXIS, axis=0, tiled=True)
    gate = jnp.dot(piece, gate_weight, preferred_element_type=jnp.float32)
    upward = jnp.dot(piece, up_weight, preferred_element_type=jnp.float32)
    hidden = (jax.nn.silu(gate) * upward).astype(jnp.bfloat16)
    total_rows, local_width = hidden.shape
    devices = lax.axis_size(AXIS)
    local_walsh = down_scales.shape[0]
    group = down_codes.shape[0] // local_walsh
    blocks = hidden.astype(jnp.float32).reshape(total_rows, local_walsh, group)
    small_table = jnp.asarray(hadamard_small(), jnp.float32)
    local_table = jnp.asarray(walsh(local_walsh), jnp.float32)
    blocks = jnp.einsum("tia,ac->tic", blocks, small_table, precision=lax.Precision.HIGHEST)
    blocks = jnp.einsum("ji,tic->tjc", local_table, blocks, precision=lax.Precision.HIGHEST)
    blocks = blocks.reshape(total_rows, local_width)
    position = lax.axis_index(AXIS)
    for level in range(devices.bit_length() - 1):
        partner = exchange(blocks.astype(jnp.bfloat16), 1 << level).astype(blocks.dtype)
        signed = (1 - 2 * (position >> level & 1)).astype(jnp.float32)
        blocks = partner + signed * blocks
    rotated = (blocks * (devices * local_width) ** (-0.5)).astype(jnp.bfloat16)
    summed = lax.psum_scatter(
        jnp.dot(rotated, down_weight, preferred_element_type=jnp.float32),
        AXIS,
        scatter_dimension=0,
        tiled=True,
    )
    return (floated + summed).astype(jnp.bfloat16)


def shards(tokens, norm_gain, gate_codes, *others):
    devices = lax.axis_size(AXIS)
    rows, width = tokens.shape
    local = gate_codes.shape[1]
    if devices == 8 and rows % 32 == 0 and local % 896 == 0 and width % 1024 == 0:
        return shards_piped(tokens, norm_gain, gate_codes, *others)
    return shards_plain(tokens, norm_gain, gate_codes, *others)


def solution(mesh):
    return jax.shard_map(
        shards,
        mesh=mesh,
        in_specs=(
            P(("groups", "tensor", "dp"), None),
            P(),
            P(None, "tensor"),
            P(None, "tensor"),
            P(None, "tensor"),
            P(None, "tensor"),
            P("tensor", None),
            P("tensor", None),
        ),
        out_specs=P(("groups", "tensor", "dp"), None),
        check_vma=False,
    )
```

```python
import functools
import math

import jax
import jax.numpy as jnp
import ml_dtypes
import numpy as np
from jax import lax
from jax.experimental import pallas as pl
from jax.experimental.pallas import tpu as pltpu
from jax.sharding import PartitionSpec as P

EPSILON = 1e-05
AXIS = "tensor"
MIB = 1 << 20


def hadamard_small():
    modulus = 13
    residues = [number * number % modulus for number in range(1, modulus)]
    legendre = [0] + [1 if number in residues else -1 for number in range(1, modulus)]
    conference = np.zeros((modulus + 1, modulus + 1), np.int64)
    conference[0, 1:] = 1
    conference[1:, 0] = 1
    for row in range(1, modulus + 1):
        for column in range(1, modulus + 1):
            conference[row, column] = legendre[(column - row) % modulus]
    plus_block = np.array([[1, 1], [1, -1]])
    zero_block = np.array([[1, -1], [-1, -1]])
    return np.kron(conference, plus_block) + np.kron(np.eye(modulus + 1, dtype=np.int64), zero_block)


def walsh(order):
    table = np.ones((1, 1), np.int64)
    while table.shape[0] < order:
        table = np.kron(np.array([[1, 1], [1, -1]]), table)
    return table


def exchange(value, stride):
    return lax.ppermute(value, AXIS, [(i, i ^ stride) for i in range(lax.axis_size(AXIS))])


def after(value, *earlier):
    return lax.optimization_barrier((value, earlier))[0]


def gather_tree(own, devices):
    pieces = {0: own}
    for k in sorted(range(1, devices), key=lambda k: (bin(k).count("1"), -k)):
        low = k & -k
        pieces[k] = exchange(pieces[k ^ low], low)
    return [(pieces[k], 0) for k in range(devices)]


def departure(devices):
    half = devices // 2
    return [1, 2] + list(range(devices - 1, half - 1, -1)) + list(range(3, half)) + [0]


def swap_direct(arrays):
    out = {}
    for k, array in zip(departure(len(arrays)), arrays):
        out[k] = (exchange(array, k) if k else array, 0)
    return [out[k] for k in range(len(arrays))]


def all_after(pieces, *earlier):
    arrays, places = distinct(pieces)
    arrays = after(arrays, *earlier)
    return [(arrays[at], start) for at, start in places]


def distinct(pieces):
    arrays = []
    for array, _ in [pieces[k] for k in departure(len(pieces))]:
        if not any(other is array for other in arrays):
            arrays.append(array)
    index = {id(array): at for at, array in enumerate(arrays)}
    return arrays, [(index[id(array)], start) for array, start in pieces]


SPLIT = 2


def split_blocks(height, tile, skip):
    return [
        pl.BlockSpec((height // SPLIT, tile), functools.partial(lambda part, i: (part, i + skip), part))
        for part in range(SPLIT)
    ]


def whole_blocks(arrays):
    return [pl.BlockSpec(array.shape, lambda i: (0, 0)) for array in arrays]


def norm_kernel(cuts, tokens_ref, gain_ref, *out_refs):
    floated = tokens_ref[...].astype(jnp.float32)
    inverse = lax.rsqrt(jnp.mean(floated * floated, axis=1, keepdims=True) + EPSILON)
    normed = (floated * inverse * gain_ref[...]).astype(jnp.bfloat16)
    for (row, column), out_ref in zip(cuts, out_refs):
        rows, columns = out_ref.shape
        out_ref[...] = normed[row : row + rows, column : column + columns]


def norm(tokens, gain, cuts):
    rows, width = tokens.shape
    return pl.pallas_call(
        functools.partial(norm_kernel, [cut[:2] for cut in cuts]),
        out_shape=[jax.ShapeDtypeStruct(cut[2:], jnp.bfloat16) for cut in cuts],
        compiler_params=pltpu.CompilerParams(vmem_limit_bytes=16 * MIB),
        cost_estimate=pl.CostEstimate(
            flops=5 * rows * width, bytes_accessed=4 * rows * width, transcendentals=rows
        ),
        name="norm",
    )(tokens, gain.reshape(1, width))


def gate_up_kernel(places, devices, rows, depth, qblock, ins, *refs):
    piece_refs = refs[:ins]
    code_refs = refs[ins : ins + 2 * SPLIT]
    gate_scale_ref, up_scale_ref = refs[ins + 2 * SPLIT : ins + 2 * SPLIT + 2]
    out_refs = refs[ins + 2 * SPLIT + 2 : -1]
    held = refs[-1]
    span = code_refs[0].shape[0]

    @pl.when(pl.program_id(0) == 0)
    def _():
        for k, (at, start) in enumerate(places):
            held[k * rows : (k + 1) * rows, :] = piece_refs[at][start : start + rows, :]

    def weight(refs_of_codes, scales, at):
        parts = []
        for row in range(at, at + depth, qblock):
            codes = refs_of_codes[row // span][row % span : row % span + qblock, :]
            step = scales[row // qblock : row // qblock + 1, :]
            parts.append((codes.astype(jnp.float32) * step).astype(jnp.bfloat16))
        return jnp.concatenate(parts, axis=0)

    gate = up = None
    for at in range(0, SPLIT * span, depth):
        left = held[:, at : at + depth]
        right = weight(code_refs[:SPLIT], gate_scale_ref, at)
        term = jnp.dot(left, right, preferred_element_type=jnp.float32)
        gate = term if gate is None else gate + term
        right = weight(code_refs[SPLIT:], up_scale_ref, at)
        term = jnp.dot(left, right, preferred_element_type=jnp.float32)
        up = term if up is None else up + term
    hidden = (gate / (1.0 + jnp.exp(-gate)) * up).astype(jnp.bfloat16)
    for k, out_ref in zip(departure(devices), out_refs):
        out_ref[...] = hidden[k * rows : (k + 1) * rows]


def gate_up(pieces, rows, gate_codes, gate_scales, up_codes, up_scales):
    devices = len(pieces)
    arrays, places = distinct(pieces)
    width, local = gate_codes.shape
    blocks = gate_scales.shape[0]
    tile = 256
    codes = split_blocks(width, tile, 0)
    scales = pl.BlockSpec((blocks, tile), lambda i: (0, i))
    return pl.pallas_call(
        functools.partial(
            gate_up_kernel, places, devices, rows, 512, width // blocks, len(arrays)
        ),
        grid=(local // tile,),
        in_specs=whole_blocks(arrays) + codes + codes + [scales, scales],
        out_specs=[pl.BlockSpec((rows, tile), lambda i: (0, i))] * devices,
        out_shape=[jax.ShapeDtypeStruct((rows, local), jnp.bfloat16)] * devices,
        scratch_shapes=[pltpu.VMEM((devices * rows, width), jnp.bfloat16)],
        compiler_params=pltpu.CompilerParams(
            dimension_semantics=("arbitrary",), vmem_limit_bytes=28 * MIB
        ),
        cost_estimate=pl.CostEstimate(
            flops=4 * devices * rows * width * local,
            bytes_accessed=4 * width * local,
            transcendentals=devices * rows * local,
        ),
        name="gate_up",
    )(*arrays, *[gate_codes] * SPLIT, *[up_codes] * SPLIT, gate_scales, up_scales)


def rotate_kernel(places, rows, factor, ins, sign_ref, *refs):
    devices = len(places)
    piece_refs = refs[:ins]
    table_ref = refs[ins]
    out_refs = dict(zip(departure(devices), refs[ins + 1 : -1]))
    held = refs[-1]
    local = piece_refs[0].shape[1]
    block = table_ref.shape[0]
    inner = local // block
    count = devices * inner
    for k, (source, start) in enumerate(places):
        sign = sign_ref[0, k].astype(jnp.bfloat16)
        for q in range(inner):
            at = (k * inner + q) * rows
            held[at : at + rows, :] = (
                piece_refs[source][start : start + rows, q * block : (q + 1) * block] * sign
            )
    for start in range(0, block, 256):
        stop = min(start + 256, block)
        product = jnp.dot(
            held[...], table_ref[:, start:stop], preferred_element_type=jnp.float32
        )
        values = [product[index * rows : (index + 1) * rows] for index in range(count)]
        stride = 1
        while stride < count:
            values = [
                values[index] + values[index ^ stride]
                if not index & stride
                else values[index ^ stride] - values[index]
                for index in range(count)
            ]
            stride *= 2
        for k in range(devices):
            scale = sign_ref[1, k] * factor
            for q in range(inner):
                out_refs[k][:, q * block + start : q * block + stop] = (
                    values[k * inner + q] * scale
                ).astype(jnp.bfloat16)


def rotate(pieces, rows, signs, table):
    devices = len(pieces)
    arrays, places = distinct(pieces)
    local = arrays[0].shape[1]
    block = table.shape[0]
    vmem = pl.BlockSpec(memory_space=pltpu.VMEM)
    return pl.pallas_call(
        functools.partial(
            rotate_kernel, places, rows, (devices * local) ** (-0.5), len(arrays)
        ),
        in_specs=[pl.BlockSpec(memory_space=pltpu.SMEM)] + [vmem] * (len(arrays) + 1),
        out_specs=[vmem] * devices,
        out_shape=[jax.ShapeDtypeStruct((rows, local), jnp.bfloat16)] * devices,
        scratch_shapes=[pltpu.VMEM((devices * rows * local // block, block), jnp.bfloat16)],
        compiler_params=pltpu.CompilerParams(vmem_limit_bytes=20 * MIB),
        cost_estimate=pl.CostEstimate(
            flops=2 * devices * rows * local * block,
            bytes_accessed=4 * devices * rows * local,
            transcendentals=devices * rows * local,
        ),
        name="rotate",
    )(signs, *arrays, table)


def down_kernel(places, rows, group, order, ins, *refs):
    devices = len(places)
    piece_refs = refs[:ins]
    code_refs = refs[ins : ins + SPLIT]
    scale_ref, keep_ref, send_ref, held, weight = refs[ins + SPLIT :]
    half = devices // 2

    @pl.when(pl.program_id(0) == 0)
    def _():
        for place, k in enumerate(order):
            at, start = places[k]
            held[place * rows : (place + 1) * rows, :] = piece_refs[at][start : start + rows, :]

    depth, tile = code_refs[0].shape
    repeat = math.lcm(group, 16)
    low_rows = lax.broadcasted_iota(jnp.int32, (8, tile), 0)
    total = None
    for part in range(SPLIT):
        for at in range(part * depth, (part + 1) * depth, repeat):
            steps = []
            for row in range(at, at + repeat, 8):
                first, last = row // group, (row + 7) // group
                step = jnp.broadcast_to(scale_ref[first : first + 1, :], (8, tile))
                if last != first:
                    other = jnp.broadcast_to(scale_ref[last : last + 1, :], (8, tile))
                    step = jnp.where(low_rows < last * group - row, step, other)
                steps.append(step)
            low = at - part * depth
            codes = code_refs[part][low : low + repeat, :].astype(jnp.float32)
            weight[at : at + repeat, :] = (codes * jnp.concatenate(steps, axis=0)).astype(
                jnp.bfloat16
            )
        term = jnp.dot(
            held[:, part * depth : (part + 1) * depth],
            weight[part * depth : (part + 1) * depth, :],
            preferred_element_type=jnp.float32,
        )
        total = term if total is None else total + term
    keep_ref[...] = total[: half * rows]
    send_ref[...] = total[half * rows :].astype(jnp.bfloat16)


def down(pieces, rows, strides, first_column, columns, codes, scales):
    devices = len(pieces)
    arrays, places = distinct(pieces)
    local = codes.shape[0]
    blocks = scales.shape[0]
    tile = 512
    skip = first_column // tile
    levels = len(strides)
    order = sorted(
        range(devices),
        key=lambda k: sum(1 << (levels - 1 - i) for i, stride in enumerate(strides) if k & stride),
    )
    out_rows = devices // 2 * rows
    return pl.pallas_call(
        functools.partial(down_kernel, places, rows, local // blocks, order, len(arrays)),
        grid=(columns // tile,),
        in_specs=whole_blocks(arrays)
        + split_blocks(local, tile, skip)
        + [pl.BlockSpec((blocks, tile), lambda i: (0, i + skip))],
        out_specs=[pl.BlockSpec((out_rows, tile), lambda i: (0, i))] * 2,
        out_shape=[
            jax.ShapeDtypeStruct((out_rows, columns), jnp.float32),
            jax.ShapeDtypeStruct((out_rows, columns), jnp.bfloat16),
        ],
        scratch_shapes=[
            pltpu.VMEM((devices * rows, local), jnp.bfloat16),
            pltpu.VMEM((local, tile), jnp.bfloat16),
        ],
        compiler_params=pltpu.CompilerParams(
            dimension_semantics=("arbitrary",), vmem_limit_bytes=24 * MIB
        ),
        cost_estimate=pl.CostEstimate(
            flops=2 * devices * rows * columns * local,
            bytes_accessed=2 * columns * local,
            transcendentals=0,
        ),
        name="down",
    )(*arrays, *[codes] * SPLIT, scales)


def add_share(shares, stride, *earlier):
    keep, send = shares
    return keep + after(exchange(send, stride), *earlier).astype(jnp.float32)


def split_share(total):
    half = total.shape[0] // 2
    return total[:half], total[half:].astype(jnp.bfloat16)


def block_order(local, group):
    order = local // group
    while order > 32:
        order //= 2
    return order


def shards_piped(
    tokens, norm_gain, gate_codes, gate_scales, up_codes, up_scales, down_codes, down_scales
):
    devices = lax.axis_size(AXIS)
    width = tokens.shape[1]
    local = gate_codes.shape[1]
    group = down_codes.shape[0] // down_scales.shape[0]
    rows = tokens.shape[0] // 2
    table = np.kron(walsh(block_order(local, group)), hadamard_small())
    table = jnp.asarray(table.astype(ml_dtypes.bfloat16))

    grid = walsh(devices)
    both = np.stack(
        [[grid[me], [grid[me ^ k, me] for k in range(devices)]] for me in range(devices)]
    )
    signs = lax.dynamic_index_in_dim(
        jnp.asarray(both, jnp.float32), lax.axis_index(AXIS), 0, keepdims=False
    )
    weights = (gate_codes, gate_scales, up_codes, up_scales)

    half = width // 2
    most = max(half, width // 512 * 5 // 8 * 512)
    own = norm(tokens, norm_gain, [(0, 0, rows, width), (rows, 0, rows, width)])
    first, second = [gather_tree(piece, devices) for piece in own]

    arrays = gate_up(first, rows, *weights)
    hidden = swap_direct(arrays)
    later_arrays = gate_up(all_after(second, arrays[-1]), rows, *weights)
    later_hidden = swap_direct(later_arrays)

    arrays = rotate(all_after(hidden, later_arrays[-1]), rows, signs, table)
    rotated = swap_direct(arrays)
    later_arrays = rotate(all_after(later_hidden, arrays[-1]), rows, signs, table)
    later_rotated = swap_direct(later_arrays)

    def contract(pieces, strides, first_column, columns):
        return down(pieces, rows, strides, first_column, columns, down_codes, down_scales)

    order, other = [1, 2, 4], [2, 1, 4]
    rotated = all_after(rotated, later_arrays[-1])
    top_left = contract(rotated, order, 0, half)
    top_right = contract(all_after(rotated, top_left[1]), other, half, half)
    left = contract(all_after(later_rotated, top_right[1]), order, 0, most)
    top_left = split_share(add_share(top_left, order[0], left[1]))
    top_right = split_share(add_share(top_right, other[0], left[1]))
    right = contract(
        all_after(later_rotated, left[1], top_left[1], top_right[1]), other, most, width - most
    )
    left = split_share(add_share(left, order[0], right[1]))
    top_left = split_share(add_share(top_left, order[1], left[1]))
    top_right = split_share(add_share(top_right, other[1], left[1]))
    right = split_share(add_share(right, other[0], top_left[1], top_right[1]))
    left = split_share(add_share(left, order[1], right[1]))
    right = split_share(add_share(right, other[1], left[1]))
    top_left = add_share(top_left, order[2], right[1])
    top_right = add_share(top_right, other[2], right[1])
    left = add_share(left, order[2], top_left, top_right)
    right = add_share(right, other[2], left)
    above = jnp.concatenate([top_left, top_right], axis=1)
    below = jnp.concatenate([left, right], axis=1)
    total = jnp.concatenate([above, below], axis=0)
    return (tokens.astype(jnp.float32) + total).astype(jnp.bfloat16)


def dequantize(codes, scales):
    blocks = scales.shape[0]
    height, width = codes.shape
    spread = codes.astype(jnp.float32).reshape(blocks, height // blocks, width) * scales[:, None, :]
    return spread.reshape(height, width).astype(jnp.bfloat16)


def shards_plain(
    tokens, norm_gain, gate_codes, gate_scales, up_codes, up_scales, down_codes, down_scales
):
    floated = tokens.astype(jnp.float32)
    normed = (
        floated
        * lax.rsqrt(jnp.mean(floated * floated, axis=1, keepdims=True) + EPSILON)
        * norm_gain
    ).astype(jnp.bfloat16)
    gate_weight = dequantize(gate_codes, gate_scales)
    up_weight = dequantize(up_codes, up_scales)
    down_weight = dequantize(down_codes, down_scales)
    piece = lax.all_gather(normed, AXIS, axis=0, tiled=True)
    gate = jnp.dot(piece, gate_weight, preferred_element_type=jnp.float32)
    upward = jnp.dot(piece, up_weight, preferred_element_type=jnp.float32)
    hidden = (jax.nn.silu(gate) * upward).astype(jnp.bfloat16)
    total_rows, local_width = hidden.shape
    devices = lax.axis_size(AXIS)
    local_walsh = down_scales.shape[0]
    group = down_codes.shape[0] // local_walsh
    blocks = hidden.astype(jnp.float32).reshape(total_rows, local_walsh, group)
    small_table = jnp.asarray(hadamard_small(), jnp.float32)
    local_table = jnp.asarray(walsh(local_walsh), jnp.float32)
    blocks = jnp.einsum("tia,ac->tic", blocks, small_table, precision=lax.Precision.HIGHEST)
    blocks = jnp.einsum("ji,tic->tjc", local_table, blocks, precision=lax.Precision.HIGHEST)
    blocks = blocks.reshape(total_rows, local_width)
    position = lax.axis_index(AXIS)
    for level in range(devices.bit_length() - 1):
        partner = exchange(blocks.astype(jnp.bfloat16), 1 << level).astype(blocks.dtype)
        signed = (1 - 2 * (position >> level & 1)).astype(jnp.float32)
        blocks = partner + signed * blocks
    rotated = (blocks * (devices * local_width) ** (-0.5)).astype(jnp.bfloat16)
    summed = lax.psum_scatter(
        jnp.dot(rotated, down_weight, preferred_element_type=jnp.float32),
        AXIS,
        scatter_dimension=0,
        tiled=True,
    )
    return (floated + summed).astype(jnp.bfloat16)


def shards(tokens, norm_gain, gate_codes, *others):
    devices = lax.axis_size(AXIS)
    rows, width = tokens.shape
    local = gate_codes.shape[1]
    if devices == 8 and rows % 32 == 0 and local % 896 == 0 and width % 1024 == 0:
        return shards_piped(tokens, norm_gain, gate_codes, *others)
    return shards_plain(tokens, norm_gain, gate_codes, *others)


def solution(mesh):
    return jax.shard_map(
        shards,
        mesh=mesh,
        in_specs=(
            P(("groups", "tensor", "dp"), None),
            P(),
            P(None, "tensor"),
            P(None, "tensor"),
            P(None, "tensor"),
            P(None, "tensor"),
            P("tensor", None),
            P("tensor", None),
        ),
        out_specs=P(("groups", "tensor", "dp"), None),
        check_vma=False,
    )
```

```python
import functools
import math

import jax
import jax.numpy as jnp
import ml_dtypes
import numpy as np
from jax import lax
from jax.experimental import pallas as pl
from jax.experimental.pallas import tpu as pltpu
from jax.sharding import PartitionSpec as P

EPSILON = 1e-05
AXIS = "tensor"
MIB = 1 << 20


def hadamard_small():
    modulus = 13
    residues = [number * number % modulus for number in range(1, modulus)]
    legendre = [0] + [1 if number in residues else -1 for number in range(1, modulus)]
    conference = np.zeros((modulus + 1, modulus + 1), np.int64)
    conference[0, 1:] = 1
    conference[1:, 0] = 1
    for row in range(1, modulus + 1):
        for column in range(1, modulus + 1):
            conference[row, column] = legendre[(column - row) % modulus]
    plus_block = np.array([[1, 1], [1, -1]])
    zero_block = np.array([[1, -1], [-1, -1]])
    return np.kron(conference, plus_block) + np.kron(np.eye(modulus + 1, dtype=np.int64), zero_block)


def walsh(order):
    table = np.ones((1, 1), np.int64)
    while table.shape[0] < order:
        table = np.kron(np.array([[1, 1], [1, -1]]), table)
    return table


def exchange(value, stride):
    return lax.ppermute(value, AXIS, [(i, i ^ stride) for i in range(lax.axis_size(AXIS))])


def after(value, *earlier):
    return lax.optimization_barrier((value, earlier))[0]


def gather_tree(own, devices):
    pieces = {0: own}
    for k in sorted(range(1, devices), key=lambda k: (bin(k).count("1"), -k)):
        low = k & -k
        pieces[k] = exchange(pieces[k ^ low], low)
    return [(pieces[k], 0) for k in range(devices)]


def gather_doubling(own, strides):
    rows = own.shape[0]
    held, places = own, {0: 0}
    for stride in strides[:-1]:
        places.update({k ^ stride: place + len(places) for k, place in places.items()})
        held = jnp.concatenate([held, exchange(held, stride)], axis=0)
    came = exchange(held, strides[-1])
    pieces = {k: (held, place * rows) for k, place in places.items()}
    pieces.update({k ^ strides[-1]: (came, place * rows) for k, place in places.items()})
    return [pieces[k] for k in range(len(pieces))]


def departure(devices):
    half = devices // 2
    return [1, 2] + list(range(devices - 1, half - 1, -1)) + list(range(3, half)) + [0]


def swap_direct(arrays):
    out = {}
    for k, array in zip(departure(len(arrays)), arrays):
        out[k] = (exchange(array, k) if k else array, 0)
    return [out[k] for k in range(len(arrays))]


def all_after(pieces, *earlier):
    arrays, places = distinct(pieces)
    arrays = after(arrays, *earlier)
    return [(arrays[at], start) for at, start in places]


def distinct(pieces):
    arrays = []
    for array, _ in [pieces[k] for k in departure(len(pieces))]:
        if not any(other is array for other in arrays):
            arrays.append(array)
    index = {id(array): at for at, array in enumerate(arrays)}
    return arrays, [(index[id(array)], start) for array, start in pieces]


SPLIT = 2


def split_blocks(height, tile, skip):
    return [
        pl.BlockSpec((height // SPLIT, tile), functools.partial(lambda part, i: (part, i + skip), part))
        for part in range(SPLIT)
    ]


def whole_blocks(arrays):
    return [pl.BlockSpec(array.shape, lambda i: (0, 0)) for array in arrays]


def norm_kernel(cuts, tokens_ref, gain_ref, *out_refs):
    floated = tokens_ref[...].astype(jnp.float32)
    inverse = lax.rsqrt(jnp.mean(floated * floated, axis=1, keepdims=True) + EPSILON)
    normed = (floated * inverse * gain_ref[...]).astype(jnp.bfloat16)
    for (row, column), out_ref in zip(cuts, out_refs):
        rows, columns = out_ref.shape
        out_ref[...] = normed[row : row + rows, column : column + columns]


def norm(tokens, gain, cuts):
    rows, width = tokens.shape
    return pl.pallas_call(
        functools.partial(norm_kernel, [cut[:2] for cut in cuts]),
        out_shape=[jax.ShapeDtypeStruct(cut[2:], jnp.bfloat16) for cut in cuts],
        compiler_params=pltpu.CompilerParams(vmem_limit_bytes=16 * MIB),
        cost_estimate=pl.CostEstimate(
            flops=5 * rows * width, bytes_accessed=4 * rows * width, transcendentals=rows
        ),
        name="norm",
    )(tokens, gain.reshape(1, width))


def gate_up_kernel(places, devices, rows, depth, qblock, ins, *refs):
    piece_refs = refs[:ins]
    code_refs = refs[ins : ins + 2 * SPLIT]
    gate_scale_ref, up_scale_ref = refs[ins + 2 * SPLIT : ins + 2 * SPLIT + 2]
    out_refs = refs[ins + 2 * SPLIT + 2 : -1]
    held = refs[-1]
    span = code_refs[0].shape[0]

    @pl.when(pl.program_id(0) == 0)
    def _():
        for k, (at, start) in enumerate(places):
            held[k * rows : (k + 1) * rows, :] = piece_refs[at][start : start + rows, :]

    def weight(refs_of_codes, scales, at):
        parts = []
        for row in range(at, at + depth, qblock):
            codes = refs_of_codes[row // span][row % span : row % span + qblock, :]
            step = scales[row // qblock : row // qblock + 1, :]
            parts.append((codes.astype(jnp.float32) * step).astype(jnp.bfloat16))
        return jnp.concatenate(parts, axis=0)

    gate = up = None
    for at in range(0, SPLIT * span, depth):
        left = held[:, at : at + depth]
        right = weight(code_refs[:SPLIT], gate_scale_ref, at)
        term = jnp.dot(left, right, preferred_element_type=jnp.float32)
        gate = term if gate is None else gate + term
        right = weight(code_refs[SPLIT:], up_scale_ref, at)
        term = jnp.dot(left, right, preferred_element_type=jnp.float32)
        up = term if up is None else up + term
    hidden = (gate / (1.0 + jnp.exp(-gate)) * up).astype(jnp.bfloat16)
    for k, out_ref in zip(departure(devices), out_refs):
        out_ref[...] = hidden[k * rows : (k + 1) * rows]


def gate_up(pieces, rows, gate_codes, gate_scales, up_codes, up_scales):
    devices = len(pieces)
    arrays, places = distinct(pieces)
    width, local = gate_codes.shape
    blocks = gate_scales.shape[0]
    tile = 512
    codes = split_blocks(width, tile, 0)
    scales = pl.BlockSpec((blocks, tile), lambda i: (0, i))
    return pl.pallas_call(
        functools.partial(
            gate_up_kernel, places, devices, rows, 512, width // blocks, len(arrays)
        ),
        grid=(local // tile,),
        in_specs=whole_blocks(arrays) + codes + codes + [scales, scales],
        out_specs=[pl.BlockSpec((rows, tile), lambda i: (0, i))] * devices,
        out_shape=[jax.ShapeDtypeStruct((rows, local), jnp.bfloat16)] * devices,
        scratch_shapes=[pltpu.VMEM((devices * rows, width), jnp.bfloat16)],
        compiler_params=pltpu.CompilerParams(
            dimension_semantics=("arbitrary",), vmem_limit_bytes=36 * MIB
        ),
        cost_estimate=pl.CostEstimate(
            flops=4 * devices * rows * width * local,
            bytes_accessed=4 * width * local,
            transcendentals=devices * rows * local,
        ),
        name="gate_up",
    )(*arrays, *[gate_codes] * SPLIT, *[up_codes] * SPLIT, gate_scales, up_scales)


def rotate_kernel(places, rows, factor, ins, sign_ref, *refs):
    devices = len(places)
    piece_refs = refs[:ins]
    table_ref = refs[ins]
    out_refs = dict(zip(departure(devices), refs[ins + 1 : -1]))
    held = refs[-1]
    local = piece_refs[0].shape[1]
    block = table_ref.shape[0]
    inner = local // block
    count = devices * inner
    for k, (source, start) in enumerate(places):
        sign = sign_ref[0, k].astype(jnp.bfloat16)
        for q in range(inner):
            at = (k * inner + q) * rows
            held[at : at + rows, :] = (
                piece_refs[source][start : start + rows, q * block : (q + 1) * block] * sign
            )
    for start in range(0, block, 256):
        stop = min(start + 256, block)
        product = jnp.dot(
            held[...], table_ref[:, start:stop], preferred_element_type=jnp.float32
        )
        values = [product[index * rows : (index + 1) * rows] for index in range(count)]
        stride = 1
        while stride < count:
            values = [
                values[index] + values[index ^ stride]
                if not index & stride
                else values[index ^ stride] - values[index]
                for index in range(count)
            ]
            stride *= 2
        for k in range(devices):
            scale = sign_ref[1, k] * factor
            for q in range(inner):
                out_refs[k][:, q * block + start : q * block + stop] = (
                    values[k * inner + q] * scale
                ).astype(jnp.bfloat16)


def rotate(pieces, rows, signs, table):
    devices = len(pieces)
    arrays, places = distinct(pieces)
    local = arrays[0].shape[1]
    block = table.shape[0]
    vmem = pl.BlockSpec(memory_space=pltpu.VMEM)
    return pl.pallas_call(
        functools.partial(
            rotate_kernel, places, rows, (devices * local) ** (-0.5), len(arrays)
        ),
        in_specs=[pl.BlockSpec(memory_space=pltpu.SMEM)] + [vmem] * (len(arrays) + 1),
        out_specs=[vmem] * devices,
        out_shape=[jax.ShapeDtypeStruct((rows, local), jnp.bfloat16)] * devices,
        scratch_shapes=[pltpu.VMEM((devices * rows * local // block, block), jnp.bfloat16)],
        compiler_params=pltpu.CompilerParams(vmem_limit_bytes=20 * MIB),
        cost_estimate=pl.CostEstimate(
            flops=2 * devices * rows * local * block,
            bytes_accessed=4 * devices * rows * local,
            transcendentals=devices * rows * local,
        ),
        name="rotate",
    )(signs, *arrays, table)


def down_kernel(places, rows, group, order, ins, *refs):
    devices = len(places)
    piece_refs = refs[:ins]
    code_refs = refs[ins : ins + SPLIT]
    scale_ref, keep_ref, send_ref, held, weight = refs[ins + SPLIT :]
    half = devices // 2

    @pl.when(pl.program_id(0) == 0)
    def _():
        for place, k in enumerate(order):
            at, start = places[k]
            held[place * rows : (place + 1) * rows, :] = piece_refs[at][start : start + rows, :]

    depth, tile = code_refs[0].shape
    repeat = math.lcm(group, 16)
    low_rows = lax.broadcasted_iota(jnp.int32, (8, tile), 0)
    total = None
    for part in range(SPLIT):
        for at in range(part * depth, (part + 1) * depth, repeat):
            steps = []
            for row in range(at, at + repeat, 8):
                first, last = row // group, (row + 7) // group
                step = jnp.broadcast_to(scale_ref[first : first + 1, :], (8, tile))
                if last != first:
                    other = jnp.broadcast_to(scale_ref[last : last + 1, :], (8, tile))
                    step = jnp.where(low_rows < last * group - row, step, other)
                steps.append(step)
            low = at - part * depth
            codes = code_refs[part][low : low + repeat, :].astype(jnp.float32)
            weight[at : at + repeat, :] = (codes * jnp.concatenate(steps, axis=0)).astype(
                jnp.bfloat16
            )
        term = jnp.dot(
            held[:, part * depth : (part + 1) * depth],
            weight[part * depth : (part + 1) * depth, :],
            preferred_element_type=jnp.float32,
        )
        total = term if total is None else total + term
    keep_ref[...] = total[: half * rows]
    send_ref[...] = total[half * rows :].astype(jnp.bfloat16)


def down(pieces, rows, strides, first_column, columns, codes, scales):
    devices = len(pieces)
    arrays, places = distinct(pieces)
    local = codes.shape[0]
    blocks = scales.shape[0]
    tile = 512
    skip = first_column // tile
    levels = len(strides)
    order = sorted(
        range(devices),
        key=lambda k: sum(1 << (levels - 1 - i) for i, stride in enumerate(strides) if k & stride),
    )
    out_rows = devices // 2 * rows
    return pl.pallas_call(
        functools.partial(down_kernel, places, rows, local // blocks, order, len(arrays)),
        grid=(columns // tile,),
        in_specs=whole_blocks(arrays)
        + split_blocks(local, tile, skip)
        + [pl.BlockSpec((blocks, tile), lambda i: (0, i + skip))],
        out_specs=[pl.BlockSpec((out_rows, tile), lambda i: (0, i))] * 2,
        out_shape=[
            jax.ShapeDtypeStruct((out_rows, columns), jnp.float32),
            jax.ShapeDtypeStruct((out_rows, columns), jnp.bfloat16),
        ],
        scratch_shapes=[
            pltpu.VMEM((devices * rows, local), jnp.bfloat16),
            pltpu.VMEM((local, tile), jnp.bfloat16),
        ],
        compiler_params=pltpu.CompilerParams(
            dimension_semantics=("arbitrary",), vmem_limit_bytes=24 * MIB
        ),
        cost_estimate=pl.CostEstimate(
            flops=2 * devices * rows * columns * local,
            bytes_accessed=2 * columns * local,
            transcendentals=0,
        ),
        name="down",
    )(*arrays, *[codes] * SPLIT, scales)


def add_share(shares, stride, *earlier):
    keep, send = shares
    return keep + after(exchange(send, stride), *earlier).astype(jnp.float32)


def split_share(total):
    half = total.shape[0] // 2
    return total[:half], total[half:].astype(jnp.bfloat16)


def block_order(local, group):
    order = local // group
    while order > 32:
        order //= 2
    return order


def shards_piped(
    tokens, norm_gain, gate_codes, gate_scales, up_codes, up_scales, down_codes, down_scales
):
    devices = lax.axis_size(AXIS)
    width = tokens.shape[1]
    local = gate_codes.shape[1]
    group = down_codes.shape[0] // down_scales.shape[0]
    rows = tokens.shape[0] // 2
    table = np.kron(walsh(block_order(local, group)), hadamard_small())
    table = jnp.asarray(table.astype(ml_dtypes.bfloat16))

    grid = walsh(devices)
    both = np.stack(
        [[grid[me], [grid[me ^ k, me] for k in range(devices)]] for me in range(devices)]
    )
    signs = lax.dynamic_index_in_dim(
        jnp.asarray(both, jnp.float32), lax.axis_index(AXIS), 0, keepdims=False
    )
    weights = (gate_codes, gate_scales, up_codes, up_scales)

    half = width // 2
    most = max(half, width // 512 * 5 // 8 * 512)
    own = norm(tokens, norm_gain, [(0, 0, rows, width), (rows, 0, rows, width)])
    first = gather_tree(own[0], devices)
    second = gather_doubling(own[1], [4, 2, 1])

    arrays = gate_up(first, rows, *weights)
    hidden = swap_direct(arrays)
    later_arrays = gate_up(all_after(second, arrays[-1]), rows, *weights)
    later_hidden = swap_direct(later_arrays)

    arrays = rotate(all_after(hidden, later_arrays[-1]), rows, signs, table)
    rotated = swap_direct(arrays)
    later_arrays = rotate(all_after(later_hidden, arrays[-1]), rows, signs, table)
    later_rotated = swap_direct(later_arrays)

    def contract(pieces, strides, first_column, columns):
        return down(pieces, rows, strides, first_column, columns, down_codes, down_scales)

    order, other = [1, 2, 4], [2, 1, 4]
    rotated = all_after(rotated, later_arrays[-1])
    top_left = contract(rotated, order, 0, half)
    top_right = contract(all_after(rotated, top_left[1]), other, half, half)
    left = contract(all_after(later_rotated, top_right[1]), order, 0, most)
    top_left = split_share(add_share(top_left, order[0], left[1]))
    top_right = split_share(add_share(top_right, other[0], left[1]))
    right = contract(
        all_after(later_rotated, left[1], top_left[1], top_right[1]), other, most, width - most
    )
    left = split_share(add_share(left, order[0], right[1]))
    top_left = split_share(add_share(top_left, order[1], left[1]))
    top_right = split_share(add_share(top_right, other[1], left[1]))
    right = split_share(add_share(right, other[0], top_left[1], top_right[1]))
    left = split_share(add_share(left, order[1], right[1]))
    right = split_share(add_share(right, other[1], left[1]))
    top_left = add_share(top_left, order[2], right[1])
    top_right = add_share(top_right, other[2], right[1])
    left = add_share(left, order[2], top_left, top_right)
    right = add_share(right, other[2], left)
    above = jnp.concatenate([top_left, top_right], axis=1)
    below = jnp.concatenate([left, right], axis=1)
    total = jnp.concatenate([above, below], axis=0)
    return (tokens.astype(jnp.float32) + total).astype(jnp.bfloat16)


def dequantize(codes, scales):
    blocks = scales.shape[0]
    height, width = codes.shape
    spread = codes.astype(jnp.float32).reshape(blocks, height // blocks, width) * scales[:, None, :]
    return spread.reshape(height, width).astype(jnp.bfloat16)


def shards_plain(
    tokens, norm_gain, gate_codes, gate_scales, up_codes, up_scales, down_codes, down_scales
):
    floated = tokens.astype(jnp.float32)
    normed = (
        floated
        * lax.rsqrt(jnp.mean(floated * floated, axis=1, keepdims=True) + EPSILON)
        * norm_gain
    ).astype(jnp.bfloat16)
    gate_weight = dequantize(gate_codes, gate_scales)
    up_weight = dequantize(up_codes, up_scales)
    down_weight = dequantize(down_codes, down_scales)
    piece = lax.all_gather(normed, AXIS, axis=0, tiled=True)
    gate = jnp.dot(piece, gate_weight, preferred_element_type=jnp.float32)
    upward = jnp.dot(piece, up_weight, preferred_element_type=jnp.float32)
    hidden = (jax.nn.silu(gate) * upward).astype(jnp.bfloat16)
    total_rows, local_width = hidden.shape
    devices = lax.axis_size(AXIS)
    local_walsh = down_scales.shape[0]
    group = down_codes.shape[0] // local_walsh
    blocks = hidden.astype(jnp.float32).reshape(total_rows, local_walsh, group)
    small_table = jnp.asarray(hadamard_small(), jnp.float32)
    local_table = jnp.asarray(walsh(local_walsh), jnp.float32)
    blocks = jnp.einsum("tia,ac->tic", blocks, small_table, precision=lax.Precision.HIGHEST)
    blocks = jnp.einsum("ji,tic->tjc", local_table, blocks, precision=lax.Precision.HIGHEST)
    blocks = blocks.reshape(total_rows, local_width)
    position = lax.axis_index(AXIS)
    for level in range(devices.bit_length() - 1):
        partner = exchange(blocks.astype(jnp.bfloat16), 1 << level).astype(blocks.dtype)
        signed = (1 - 2 * (position >> level & 1)).astype(jnp.float32)
        blocks = partner + signed * blocks
    rotated = (blocks * (devices * local_width) ** (-0.5)).astype(jnp.bfloat16)
    summed = lax.psum_scatter(
        jnp.dot(rotated, down_weight, preferred_element_type=jnp.float32),
        AXIS,
        scatter_dimension=0,
        tiled=True,
    )
    return (floated + summed).astype(jnp.bfloat16)


def shards(tokens, norm_gain, gate_codes, *others):
    devices = lax.axis_size(AXIS)
    rows, width = tokens.shape
    local = gate_codes.shape[1]
    if devices == 8 and rows % 32 == 0 and local % 896 == 0 and width % 1024 == 0:
        return shards_piped(tokens, norm_gain, gate_codes, *others)
    return shards_plain(tokens, norm_gain, gate_codes, *others)


def solution(mesh):
    return jax.shard_map(
        shards,
        mesh=mesh,
        in_specs=(
            P(("groups", "tensor", "dp"), None),
            P(),
            P(None, "tensor"),
            P(None, "tensor"),
            P(None, "tensor"),
            P(None, "tensor"),
            P("tensor", None),
            P("tensor", None),
        ),
        out_specs=P(("groups", "tensor", "dp"), None),
        check_vma=False,
    )
```

```python
import functools
import math

import jax
import jax.numpy as jnp
import ml_dtypes
import numpy as np
from jax import lax
from jax.experimental import pallas as pl
from jax.experimental.pallas import tpu as pltpu
from jax.sharding import PartitionSpec as P

EPSILON = 1e-05
AXIS = "tensor"
MIB = 1 << 20


def hadamard_small():
    modulus = 13
    residues = [number * number % modulus for number in range(1, modulus)]
    legendre = [0] + [1 if number in residues else -1 for number in range(1, modulus)]
    conference = np.zeros((modulus + 1, modulus + 1), np.int64)
    conference[0, 1:] = 1
    conference[1:, 0] = 1
    for row in range(1, modulus + 1):
        for column in range(1, modulus + 1):
            conference[row, column] = legendre[(column - row) % modulus]
    plus_block = np.array([[1, 1], [1, -1]])
    zero_block = np.array([[1, -1], [-1, -1]])
    return np.kron(conference, plus_block) + np.kron(np.eye(modulus + 1, dtype=np.int64), zero_block)


def walsh(order):
    table = np.ones((1, 1), np.int64)
    while table.shape[0] < order:
        table = np.kron(np.array([[1, 1], [1, -1]]), table)
    return table


def exchange(value, stride):
    return lax.ppermute(value, AXIS, [(i, i ^ stride) for i in range(lax.axis_size(AXIS))])


def after(value, *earlier):
    return lax.optimization_barrier((value, earlier))[0]


def gather_tree(own, devices):
    pieces = {0: own}
    for k in sorted(range(1, devices), key=lambda k: (bin(k).count("1"), -k)):
        low = k & -k
        pieces[k] = exchange(pieces[k ^ low], low)
    return [(pieces[k], 0) for k in range(devices)]


def departure(devices):
    half = devices // 2
    return [1, 2] + list(range(devices - 1, half - 1, -1)) + list(range(3, half)) + [0]


def swap_direct(arrays):
    out = {}
    for k, array in zip(departure(len(arrays)), arrays):
        out[k] = (exchange(array, k) if k else array, 0)
    return [out[k] for k in range(len(arrays))]


def all_after(pieces, *earlier):
    arrays, places = distinct(pieces)
    arrays = after(arrays, *earlier)
    return [(arrays[at], start) for at, start in places]


def distinct(pieces):
    arrays = []
    for array, _ in [pieces[k] for k in departure(len(pieces))]:
        if not any(other is array for other in arrays):
            arrays.append(array)
    index = {id(array): at for at, array in enumerate(arrays)}
    return arrays, [(index[id(array)], start) for array, start in pieces]


SPLIT = 2


def split_blocks(height, tile, skip):
    return [
        pl.BlockSpec((height // SPLIT, tile), functools.partial(lambda part, i: (part, i + skip), part))
        for part in range(SPLIT)
    ]


def whole_blocks(arrays):
    return [pl.BlockSpec(array.shape, lambda i: (0, 0)) for array in arrays]


def norm_kernel(cuts, tokens_ref, gain_ref, *out_refs):
    floated = tokens_ref[...].astype(jnp.float32)
    inverse = lax.rsqrt(jnp.mean(floated * floated, axis=1, keepdims=True) + EPSILON)
    normed = (floated * inverse * gain_ref[...]).astype(jnp.bfloat16)
    for (row, column), out_ref in zip(cuts, out_refs):
        rows, columns = out_ref.shape
        out_ref[...] = normed[row : row + rows, column : column + columns]


def norm(tokens, gain, cuts):
    rows, width = tokens.shape
    return pl.pallas_call(
        functools.partial(norm_kernel, [cut[:2] for cut in cuts]),
        out_shape=[jax.ShapeDtypeStruct(cut[2:], jnp.bfloat16) for cut in cuts],
        compiler_params=pltpu.CompilerParams(vmem_limit_bytes=16 * MIB),
        cost_estimate=pl.CostEstimate(
            flops=5 * rows * width, bytes_accessed=4 * rows * width, transcendentals=rows
        ),
        name="norm",
    )(tokens, gain.reshape(1, width))


def gate_up_kernel(places, devices, rows, depth, qblock, ins, *refs):
    piece_refs = refs[:ins]
    code_refs = refs[ins : ins + 2 * SPLIT]
    gate_scale_ref, up_scale_ref = refs[ins + 2 * SPLIT : ins + 2 * SPLIT + 2]
    out_refs = refs[ins + 2 * SPLIT + 2 : -1]
    held = refs[-1]
    span = code_refs[0].shape[0]

    @pl.when(pl.program_id(0) == 0)
    def _():
        for k, (at, start) in enumerate(places):
            held[k * rows : (k + 1) * rows, :] = piece_refs[at][start : start + rows, :]

    def weight(refs_of_codes, scales, at):
        parts = []
        for row in range(at, at + depth, qblock):
            codes = refs_of_codes[row // span][row % span : row % span + qblock, :]
            step = scales[row // qblock : row // qblock + 1, :]
            parts.append((codes.astype(jnp.float32) * step).astype(jnp.bfloat16))
        return jnp.concatenate(parts, axis=0)

    gate = up = None
    for at in range(0, SPLIT * span, depth):
        left = held[:, at : at + depth]
        right = weight(code_refs[:SPLIT], gate_scale_ref, at)
        term = jnp.dot(left, right, preferred_element_type=jnp.float32)
        gate = term if gate is None else gate + term
        right = weight(code_refs[SPLIT:], up_scale_ref, at)
        term = jnp.dot(left, right, preferred_element_type=jnp.float32)
        up = term if up is None else up + term
    hidden = (gate / (1.0 + jnp.exp(-gate)) * up).astype(jnp.bfloat16)
    for k, out_ref in zip(departure(devices), out_refs):
        out_ref[...] = hidden[k * rows : (k + 1) * rows]


def gate_up(pieces, rows, gate_codes, gate_scales, up_codes, up_scales):
    devices = len(pieces)
    arrays, places = distinct(pieces)
    width, local = gate_codes.shape
    blocks = gate_scales.shape[0]
    tile = 512 if local % 512 == 0 else 128
    codes = split_blocks(width, tile, 0)
    scales = pl.BlockSpec((blocks, tile), lambda i: (0, i))
    return pl.pallas_call(
        functools.partial(
            gate_up_kernel, places, devices, rows, 512, width // blocks, len(arrays)
        ),
        grid=(local // tile,),
        in_specs=whole_blocks(arrays) + codes + codes + [scales, scales],
        out_specs=[pl.BlockSpec((rows, tile), lambda i: (0, i))] * devices,
        out_shape=[jax.ShapeDtypeStruct((rows, local), jnp.bfloat16)] * devices,
        scratch_shapes=[pltpu.VMEM((devices * rows, width), jnp.bfloat16)],
        compiler_params=pltpu.CompilerParams(
            dimension_semantics=("arbitrary",), vmem_limit_bytes=36 * MIB
        ),
        cost_estimate=pl.CostEstimate(
            flops=4 * devices * rows * width * local,
            bytes_accessed=4 * width * local,
            transcendentals=devices * rows * local,
        ),
        name="gate_up",
    )(*arrays, *[gate_codes] * SPLIT, *[up_codes] * SPLIT, gate_scales, up_scales)


def rotate_kernel(places, rows, factor, ins, sign_ref, *refs):
    devices = len(places)
    piece_refs = refs[:ins]
    table_ref = refs[ins]
    out_refs = dict(zip(departure(devices), refs[ins + 1 : -1]))
    held = refs[-1]
    local = piece_refs[0].shape[1]
    block = table_ref.shape[0]
    inner = local // block
    count = devices * inner
    for k, (source, start) in enumerate(places):
        sign = sign_ref[0, k].astype(jnp.bfloat16)
        for q in range(inner):
            at = (k * inner + q) * rows
            held[at : at + rows, :] = (
                piece_refs[source][start : start + rows, q * block : (q + 1) * block] * sign
            )
    for start in range(0, block, 256):
        stop = min(start + 256, block)
        product = jnp.dot(
            held[...], table_ref[:, start:stop], preferred_element_type=jnp.float32
        )
        values = [product[index * rows : (index + 1) * rows] for index in range(count)]
        stride = 1
        while stride < count:
            values = [
                values[index] + values[index ^ stride]
                if not index & stride
                else values[index ^ stride] - values[index]
                for index in range(count)
            ]
            stride *= 2
        for k in range(devices):
            scale = sign_ref[1, k] * factor
            for q in range(inner):
                out_refs[k][:, q * block + start : q * block + stop] = (
                    values[k * inner + q] * scale
                ).astype(jnp.bfloat16)


def rotate(pieces, rows, signs, table):
    devices = len(pieces)
    arrays, places = distinct(pieces)
    local = arrays[0].shape[1]
    block = table.shape[0]
    vmem = pl.BlockSpec(memory_space=pltpu.VMEM)
    return pl.pallas_call(
        functools.partial(
            rotate_kernel, places, rows, (devices * local) ** (-0.5), len(arrays)
        ),
        in_specs=[pl.BlockSpec(memory_space=pltpu.SMEM)] + [vmem] * (len(arrays) + 1),
        out_specs=[vmem] * devices,
        out_shape=[jax.ShapeDtypeStruct((rows, local), jnp.bfloat16)] * devices,
        scratch_shapes=[pltpu.VMEM((devices * rows * local // block, block), jnp.bfloat16)],
        compiler_params=pltpu.CompilerParams(vmem_limit_bytes=20 * MIB),
        cost_estimate=pl.CostEstimate(
            flops=2 * devices * rows * local * block,
            bytes_accessed=4 * devices * rows * local,
            transcendentals=devices * rows * local,
        ),
        name="rotate",
    )(signs, *arrays, table)


def down_kernel(places, rows, group, order, ins, *refs):
    devices = len(places)
    piece_refs = refs[:ins]
    code_refs = refs[ins : ins + SPLIT]
    scale_ref, keep_ref, send_ref, held, weight = refs[ins + SPLIT :]
    half = devices // 2

    @pl.when(pl.program_id(0) == 0)
    def _():
        for place, k in enumerate(order):
            at, start = places[k]
            held[place * rows : (place + 1) * rows, :] = piece_refs[at][start : start + rows, :]

    depth, tile = code_refs[0].shape
    repeat = math.lcm(group, 16)
    low_rows = lax.broadcasted_iota(jnp.int32, (8, tile), 0)
    total = None
    for part in range(SPLIT):
        for at in range(part * depth, (part + 1) * depth, repeat):
            steps = []
            for row in range(at, at + repeat, 8):
                first, last = row // group, (row + 7) // group
                step = jnp.broadcast_to(scale_ref[first : first + 1, :], (8, tile))
                if last != first:
                    other = jnp.broadcast_to(scale_ref[last : last + 1, :], (8, tile))
                    step = jnp.where(low_rows < last * group - row, step, other)
                steps.append(step)
            low = at - part * depth
            codes = code_refs[part][low : low + repeat, :].astype(jnp.float32)
            weight[at : at + repeat, :] = (codes * jnp.concatenate(steps, axis=0)).astype(
                jnp.bfloat16
            )
        term = jnp.dot(
            held[:, part * depth : (part + 1) * depth],
            weight[part * depth : (part + 1) * depth, :],
            preferred_element_type=jnp.float32,
        )
        total = term if total is None else total + term
    keep_ref[...] = total[: half * rows]
    send_ref[...] = total[half * rows :].astype(jnp.bfloat16)


def down(pieces, rows, strides, first_column, columns, codes, scales):
    devices = len(pieces)
    arrays, places = distinct(pieces)
    local = codes.shape[0]
    blocks = scales.shape[0]
    tile = 512
    skip = first_column // tile
    levels = len(strides)
    order = sorted(
        range(devices),
        key=lambda k: sum(1 << (levels - 1 - i) for i, stride in enumerate(strides) if k & stride),
    )
    out_rows = devices // 2 * rows
    return pl.pallas_call(
        functools.partial(down_kernel, places, rows, local // blocks, order, len(arrays)),
        grid=(columns // tile,),
        in_specs=whole_blocks(arrays)
        + split_blocks(local, tile, skip)
        + [pl.BlockSpec((blocks, tile), lambda i: (0, i + skip))],
        out_specs=[pl.BlockSpec((out_rows, tile), lambda i: (0, i))] * 2,
        out_shape=[
            jax.ShapeDtypeStruct((out_rows, columns), jnp.float32),
            jax.ShapeDtypeStruct((out_rows, columns), jnp.bfloat16),
        ],
        scratch_shapes=[
            pltpu.VMEM((devices * rows, local), jnp.bfloat16),
            pltpu.VMEM((local, tile), jnp.bfloat16),
        ],
        compiler_params=pltpu.CompilerParams(
            dimension_semantics=("arbitrary",), vmem_limit_bytes=24 * MIB
        ),
        cost_estimate=pl.CostEstimate(
            flops=2 * devices * rows * columns * local,
            bytes_accessed=2 * columns * local,
            transcendentals=0,
        ),
        name="down",
    )(*arrays, *[codes] * SPLIT, scales)


def add_share(shares, stride, *earlier):
    keep, send = shares
    return keep + after(exchange(send, stride), *earlier).astype(jnp.float32)


def split_share(total):
    half = total.shape[0] // 2
    return total[:half], total[half:].astype(jnp.bfloat16)


def block_order(local, group):
    order = local // group
    while order > 32:
        order //= 2
    return order


def shards_piped(
    tokens, norm_gain, gate_codes, gate_scales, up_codes, up_scales, down_codes, down_scales
):
    devices = lax.axis_size(AXIS)
    width = tokens.shape[1]
    local = gate_codes.shape[1]
    group = down_codes.shape[0] // down_scales.shape[0]
    rows = tokens.shape[0] // 2
    table = np.kron(walsh(block_order(local, group)), hadamard_small())
    table = jnp.asarray(table.astype(ml_dtypes.bfloat16))

    grid = walsh(devices)
    both = np.stack(
        [[grid[me], [grid[me ^ k, me] for k in range(devices)]] for me in range(devices)]
    )
    signs = lax.dynamic_index_in_dim(
        jnp.asarray(both, jnp.float32), lax.axis_index(AXIS), 0, keepdims=False
    )
    weights = (gate_codes, gate_scales, up_codes, up_scales)

    half = width // 2
    most = max(half, width // 512 * 5 // 8 * 512)
    own = norm(tokens, norm_gain, [(0, 0, rows, width), (rows, 0, rows, width)])
    first, second = [gather_tree(piece, devices) for piece in own]

    arrays = gate_up(first, rows, *weights)
    hidden = swap_direct(arrays)
    later_arrays = gate_up(all_after(second, arrays[-1]), rows, *weights)
    later_hidden = swap_direct(later_arrays)

    arrays = rotate(all_after(hidden, later_arrays[-1]), rows, signs, table)
    rotated = swap_direct(arrays)
    later_arrays = rotate(all_after(later_hidden, arrays[-1]), rows, signs, table)
    later_rotated = swap_direct(later_arrays)

    def contract(pieces, strides, first_column, columns):
        return down(pieces, rows, strides, first_column, columns, down_codes, down_scales)

    order, other = [1, 2, 4], [2, 1, 4]
    rotated = all_after(rotated, later_arrays[-1])
    top_left = contract(rotated, order, 0, half)
    top_right = contract(all_after(rotated, top_left[1]), other, half, half)
    left = contract(all_after(later_rotated, top_right[1]), order, 0, most)
    top_left = split_share(add_share(top_left, order[0], left[1]))
    top_right = split_share(add_share(top_right, other[0], left[1]))
    right = contract(
        all_after(later_rotated, left[1], top_left[1], top_right[1]), other, most, width - most
    )
    left = split_share(add_share(left, order[0], right[1]))
    top_left = split_share(add_share(top_left, order[1], left[1]))
    top_right = split_share(add_share(top_right, other[1], left[1]))
    right = split_share(add_share(right, other[0], top_left[1], top_right[1]))
    left = split_share(add_share(left, order[1], right[1]))
    right = split_share(add_share(right, other[1], left[1]))
    top_left = add_share(top_left, order[2], right[1])
    top_right = add_share(top_right, other[2], right[1])
    left = add_share(left, order[2], top_left, top_right)
    right = add_share(right, other[2], left)
    above = jnp.concatenate([top_left, top_right], axis=1)
    below = jnp.concatenate([left, right], axis=1)
    total = jnp.concatenate([above, below], axis=0)
    return (tokens.astype(jnp.float32) + total).astype(jnp.bfloat16)


def dequantize(codes, scales):
    blocks = scales.shape[0]
    height, width = codes.shape
    spread = codes.astype(jnp.float32).reshape(blocks, height // blocks, width) * scales[:, None, :]
    return spread.reshape(height, width).astype(jnp.bfloat16)


def shards_plain(
    tokens, norm_gain, gate_codes, gate_scales, up_codes, up_scales, down_codes, down_scales
):
    floated = tokens.astype(jnp.float32)
    normed = (
        floated
        * lax.rsqrt(jnp.mean(floated * floated, axis=1, keepdims=True) + EPSILON)
        * norm_gain
    ).astype(jnp.bfloat16)
    gate_weight = dequantize(gate_codes, gate_scales)
    up_weight = dequantize(up_codes, up_scales)
    down_weight = dequantize(down_codes, down_scales)
    piece = lax.all_gather(normed, AXIS, axis=0, tiled=True)
    gate = jnp.dot(piece, gate_weight, preferred_element_type=jnp.float32)
    upward = jnp.dot(piece, up_weight, preferred_element_type=jnp.float32)
    hidden = (jax.nn.silu(gate) * upward).astype(jnp.bfloat16)
    total_rows, local_width = hidden.shape
    devices = lax.axis_size(AXIS)
    local_walsh = down_scales.shape[0]
    group = down_codes.shape[0] // local_walsh
    blocks = hidden.astype(jnp.float32).reshape(total_rows, local_walsh, group)
    small_table = jnp.asarray(hadamard_small(), jnp.float32)
    local_table = jnp.asarray(walsh(local_walsh), jnp.float32)
    blocks = jnp.einsum("tia,ac->tic", blocks, small_table, precision=lax.Precision.HIGHEST)
    blocks = jnp.einsum("ji,tic->tjc", local_table, blocks, precision=lax.Precision.HIGHEST)
    blocks = blocks.reshape(total_rows, local_width)
    position = lax.axis_index(AXIS)
    for level in range(devices.bit_length() - 1):
        partner = exchange(blocks.astype(jnp.bfloat16), 1 << level).astype(blocks.dtype)
        signed = (1 - 2 * (position >> level & 1)).astype(jnp.float32)
        blocks = partner + signed * blocks
    rotated = (blocks * (devices * local_width) ** (-0.5)).astype(jnp.bfloat16)
    summed = lax.psum_scatter(
        jnp.dot(rotated, down_weight, preferred_element_type=jnp.float32),
        AXIS,
        scatter_dimension=0,
        tiled=True,
    )
    return (floated + summed).astype(jnp.bfloat16)


def shards(tokens, norm_gain, gate_codes, *others):
    devices = lax.axis_size(AXIS)
    rows, width = tokens.shape
    local = gate_codes.shape[1]
    if devices == 8 and rows % 32 == 0 and local % 896 == 0 and width % 1024 == 0:
        return shards_piped(tokens, norm_gain, gate_codes, *others)
    return shards_plain(tokens, norm_gain, gate_codes, *others)


def solution(mesh):
    return jax.shard_map(
        shards,
        mesh=mesh,
        in_specs=(
            P(("groups", "tensor", "dp"), None),
            P(),
            P(None, "tensor"),
            P(None, "tensor"),
            P(None, "tensor"),
            P(None, "tensor"),
            P("tensor", None),
            P("tensor", None),
        ),
        out_specs=P(("groups", "tensor", "dp"), None),
        check_vma=False,
    )
```
